32 devices in a mesh: parts: 2 (over x), row: 16 (over z, y, core).
Axes of the slice: x: 2, y: 2, z: 4, core: 2. Of those that a mesh axis runs over, the one named last changes fastest.
Arguments:
- adj_rows: bfloat16 [6144, 32768], P(('parts', 'row')), parts along dimension 0, may hold values from 0 to 1
- adj_panel: bfloat16 [2, 32768, 384], P(None, ('parts', 'row')), parts along dimension 1, may hold values from 0 to 1
- adj_tile: bfloat16 [6144, 384], P(('parts', 'row')), parts along dimension 0, may hold values from 0 to 1
Outputs:
- intersection: float32 [6144, 384], P(('parts', 'row')), parts along dimension 0
- degree: float32 [6144], P(('parts', 'row')), parts along dimension 0
The draws below stay inside these ranges and needn't reach their ends.
There are 2 independent parts, one for each index of `parts`. The reference program is written for one: setup_inputs(seed, part) draws one part's arguments, and reference() takes and returns one part's arrays. A program takes and returns all parts, laid end to end along the dimension named above; each array names one. Nothing has to cross between parts.
All inputs are finite; a program needn't handle non-finite values.
Results may differ from the reference program's by a relative error of at most 0.0003.
Values may be sent and summed in bfloat16 or wider, within the bound.
No kernel may reach another device: no remote copies, remote signals or barrier semaphores. Data moves between devices by JAX's collectives and lax.ppermute only.
A program may use at most 128 MiB of HBM per device.

```python
import jax
import jax.numpy as jnp
from jax import lax

PANEL = 16384
SECTIONS = 2
COLS = 384
ROWS_DEV = 192
CONTRACT = 32768
GENES = 3072
N_ROW = 16


def module_labels(key):
    groups = COLS // 8
    order_rank = jax.random.permutation(jax.random.fold_in(key, 101), CONTRACT)
    gene_group = jnp.where(order_rank < 32 * groups, order_rank % groups, -1).astype(jnp.int32)
    row_group = jax.random.randint(jax.random.fold_in(key, 102), (GENES,), 0, groups).astype(jnp.int32)
    col_group = (jax.random.permutation(jax.random.fold_in(key, 103), COLS) % groups).astype(jnp.int32)
    return (gene_group, row_group, col_group)


def edge_values(uniform_draw, edge_rate, faint_scale, exponent):
    safe_rate = jnp.maximum(edge_rate, 0.001)
    strong_value = 10.0 ** (-(uniform_draw / safe_rate) ** exponent)
    remainder = jnp.clip((uniform_draw - edge_rate) / (1.0 - edge_rate), 0.0, 1.0)
    faint_value = faint_scale * 10.0 ** (2.0 * remainder ** exponent - 1.0)
    return jnp.where(uniform_draw < edge_rate, strong_value, faint_value)


def draw_adj_rows(key, part):
    gene_group, row_group, col_group = module_labels(key)
    key = jax.random.fold_in(key, 1)
    exponent = 1.0

    def block_rows(block_index):
        block_key = jax.random.fold_in(key, block_index)
        uniform_draw = jax.random.uniform(jax.random.fold_in(block_key, 0), (ROWS_DEV, CONTRACT), jnp.float32)
        scales = jax.random.uniform(jax.random.fold_in(block_key, 1), (ROWS_DEV, 2), jnp.float32)
        strong_rate = 0.15 * 6.0 ** scales[:, 0]
        row_mean = 0.2 * (0.2 * CONTRACT) ** (scales[:, 1] - 1.0)
        faint_scale = row_mean / 2.15
        groups_here = lax.dynamic_slice_in_dim(row_group, block_index * ROWS_DEV, ROWS_DEV)
        member = gene_group[None, :] == groups_here[:, None]
        edge_rate = jnp.where(member, strong_rate[:, None], 0.0)
        return edge_values(uniform_draw, edge_rate, faint_scale[:, None], exponent)
    blocks = lax.map(block_rows, jnp.arange(N_ROW, dtype=jnp.int32))
    return blocks.reshape(GENES, CONTRACT).astype(jnp.bfloat16)


def draw_adj_panel(key, part):
    gene_group, row_group, col_group = module_labels(key)
    key = jax.random.fold_in(key, 2)
    exponent = 1.0
    uniform_draw = jax.random.uniform(jax.random.fold_in(key, 0), (SECTIONS, PANEL, COLS), jnp.float32)
    scales = jax.random.uniform(jax.random.fold_in(key, 1), (2, COLS), jnp.float32)
    strong_rate = 0.15 * 6.0 ** scales[0]
    col_mean = 0.01 * 10.0 ** scales[1]
    faint_scale = col_mean / 2.15
    shard_index = jnp.arange(PANEL) // (PANEL // N_ROW)
    riser = 0.5 + shard_index.astype(jnp.float32) / max(N_ROW - 1, 1)
    section_genes = gene_group.reshape(SECTIONS, PANEL)
    member = section_genes[:, :, None] == col_group[None, None, :]
    edge_rate = jnp.where(member, strong_rate[None, None, :], 0.0)
    faint_full = faint_scale[None, None, :] * riser[None, :, None]
    return edge_values(uniform_draw, edge_rate, faint_full, exponent).astype(jnp.bfloat16)


def draw_adj_tile(key, part):
    gene_group, row_group, col_group = module_labels(key)
    key = jax.random.fold_in(key, 3)
    exponent = 1.0
    uniform_draw = jax.random.uniform(key, (GENES, COLS), jnp.float32)
    same_group = row_group[:, None] == col_group[None, :]
    edge_rate = jnp.where(same_group, 0.6, 0.1)
    return edge_values(uniform_draw, edge_rate, 0.001, exponent).astype(jnp.bfloat16)


def setup_inputs(seed: int = 0, part: int = 0) -> dict:
    splits = jax.random.split(jax.random.key(seed), 4)
    part_keys = jax.random.split(jax.random.fold_in(splits[3], part), 4)
    adj_rows = draw_adj_rows(jax.random.fold_in(jax.random.fold_in(splits[3], part), 71), part)
    adj_panel = draw_adj_panel(jax.random.fold_in(jax.random.fold_in(splits[3], part), 71), part)
    adj_tile = draw_adj_tile(jax.random.fold_in(jax.random.fold_in(splits[3], part), 71), part)
    return {"adj_rows": adj_rows, "adj_panel": adj_panel, "adj_tile": adj_tile}


def reference(adj_rows, adj_panel, adj_tile):
    degree = jnp.sum(adj_rows, axis=1, dtype=jnp.float32)
    col_degree = jnp.sum(adj_panel, axis=(0, 1), dtype=jnp.float32)
    square = jnp.zeros((adj_rows.shape[0], adj_panel.shape[2]), jnp.float32)
    for section in range(SECTIONS):
        block = adj_rows[:, section * PANEL:(section + 1) * PANEL]
        square = square + jnp.dot(block, adj_panel[section], preferred_element_type=jnp.float32)
    tile = adj_tile.astype(jnp.float32)
    lower = jnp.minimum(degree[:, None], col_degree[None, :])
    intersection = (square + tile) / (lower + 1.0 - tile)
    return intersection, degree
```

```python
import jax
import jax.numpy as jnp
import numpy as np
from jax import lax
from jax.sharding import PartitionSpec as P

CORES = 2


def chip_cycle(chips):
    wide = 1
    while (2 * wide) ** 2 <= chips:
        wide *= 2
    high = chips // wide
    if wide == 1 or high % 2 or wide * high != chips:
        return list(range(chips))
    walk = [(0, 0)]
    for i in range(high):
        line = range(1, wide)
        walk += [(i, j) for j in (line if i % 2 == 0 else reversed(line))]
    walk += [(i, 0) for i in range(high - 1, 0, -1)]
    return [i * wide + j for i, j in walk]


def make_shards(n_row):
    chips = n_row // CORES
    cycle = chip_cycle(chips)
    place = {chip: k for k, chip in enumerate(cycle)}

    def ring(step):
        return [
            (cycle[k] * CORES + c, cycle[(k + step) % chips] * CORES + c)
            for k in range(chips)
            for c in range(CORES)
        ]

    swap = [(d, d ^ 1) for d in range(n_row)]

    def owners(distance):
        return np.array([cycle[(place[d // CORES] - distance) % chips] for d in range(n_row)], np.int32)

    def shards(adj_rows, adj_panel, adj_tile):
        rows = adj_rows.shape[0]
        sections, depth, width = adj_panel.shape
        panel = n_row * depth
        me = lax.axis_index("row")
        core = lax.rem(me, CORES)

        pieces = [adj_panel[s] for s in range(sections)]
        lent = jnp.concatenate(
            [
                lax.dynamic_slice_in_dim(adj_rows, s * panel + (chip * CORES + 1 - core) * depth, depth, 1)
                for s in range(sections)
                for chip in range(chips)
            ],
            axis=1,
        )
        borrowed = lax.ppermute(lent, "row", swap)
        degree = jnp.sum(adj_rows, axis=1, dtype=jnp.float32)

        mine = jnp.zeros((rows, width), jnp.float32)
        theirs = jnp.zeros((rows, width), jnp.float32)
        col = jnp.zeros((1, width), jnp.float32)
        for step in range(chips):
            following = pieces
            if step < chips - 1:
                following = [
                    lax.ppermute(piece, "row", ring(1 if s % 2 == 0 else -1)) for s, piece in enumerate(pieces)
                ]
            for s, piece in enumerate(pieces):
                chip = jnp.asarray(owners(step if s % 2 == 0 else -step))[me]
                own = lax.dynamic_slice_in_dim(adj_rows, s * panel + (chip * CORES + core) * depth, depth, 1)
                other = lax.dynamic_slice_in_dim(borrowed, (s * chips + chip) * depth, depth, 1)
                mine = mine + jnp.dot(own, piece, preferred_element_type=jnp.float32)
                theirs = theirs + jnp.dot(other, piece, preferred_element_type=jnp.float32)
                col = col + jnp.sum(piece, axis=0, dtype=jnp.float32, keepdims=True)
            pieces = following

        partner = lax.ppermute(jnp.concatenate([theirs, jnp.broadcast_to(col, (8, width))], axis=0), "row", swap)
        square = mine + partner[:rows]
        col_degree = col + partner[rows : rows + 1]
        tile = adj_tile.astype(jnp.float32)
        lower = jnp.minimum(degree[:, None], col_degree)
        intersection = (square + tile) / (lower + 1.0 - tile)
        return (intersection, degree)

    return shards


def solution(mesh):
    in_specs = (
        P(("parts", "row"), None),
        P(None, ("parts", "row"), None),
        P(("parts", "row"), None),
    )
    out_specs = (P(("parts", "row"), None), P(("parts", "row")))
    return jax.shard_map(
        make_shards(mesh.shape["row"]), mesh=mesh, in_specs=in_specs, out_specs=out_specs, check_vma=False
    )
```

```python
import functools

import jax
import jax.numpy as jnp
import numpy as np
from jax import lax
from jax.experimental import pallas as pl
from jax.experimental.pallas import tpu as pltpu
from jax.sharding import PartitionSpec as P

CORES = 2
ONES = 16
MOST = 2
DEGREE_PARTS = 2
SHORT = pl.CostEstimate(flops=0, bytes_accessed=1024, transcendentals=0)
VMEM_LIMIT = 24 * 1024 * 1024


def chip_cycle(chips):
    wide = 1
    while (2 * wide) ** 2 <= chips:
        wide *= 2
    high = chips // wide
    if wide == 1 or high % 2 or wide * high != chips:
        return list(range(chips))
    walk = [(0, 0)]
    for i in range(high):
        line = range(1, wide)
        walk += [(i, j) for j in (line if i % 2 == 0 else reversed(line))]
    walk += [(i, 0) for i in range(high - 1, 0, -1)]
    return [i * wide + j for i, j in walk]


def lend_kernel(where, gate, *refs):
    out_ref = refs[-1]
    depth = refs[0].shape[1]
    for s, ref in enumerate(refs[:-1]):
        out_ref[:, s * depth : (s + 1) * depth] = ref[...]


def lend(where, gate, adj_rows, step, sections, n_row, depth):
    rows = adj_rows.shape[0]

    def block(s):
        return pl.BlockSpec(
            (rows, depth),
            lambda g, where: (0, s * n_row + where[1 + step * sections + s] * CORES + 1 - where[0]),
        )

    return pl.pallas_call(
        lend_kernel,
        grid_spec=pltpu.PrefetchScalarGridSpec(
            num_scalar_prefetch=1,
            grid=(1,),
            in_specs=[pl.BlockSpec(memory_space=pl.ANY)] + [block(s) for s in range(sections)],
            out_specs=pl.BlockSpec((rows, sections * depth), lambda g, where: (0, 0)),
        ),
        out_shape=jax.ShapeDtypeStruct((rows, sections * depth), adj_rows.dtype),
        compiler_params=pltpu.CompilerParams(vmem_limit_bytes=VMEM_LIMIT),
        cost_estimate=SHORT,
        name="lend",
    )(where, gate, *[adj_rows] * sections)


def absorb_kernel(sections, rows, first, where, *refs):
    own, other, slab = (refs[k * sections : (k + 1) * sections] for k in range(3))
    mine_out, theirs_out = refs[-2:]
    total = None
    for s in range(sections):
        ones = jnp.ones((ONES, own[s].shape[1]), own[s].dtype)
        left = jnp.concatenate([own[s][...], other[s][...], ones], axis=0)
        product = jnp.dot(left, slab[s][...], preferred_element_type=jnp.float32)
        total = product if total is None else total + product
    mine, theirs = total[:rows], total[rows:]
    if not first:
        mine_in, theirs_in = refs[3 * sections : 3 * sections + 2]
        mine, theirs = mine + mine_in[...], theirs + theirs_in[...]
    mine_out[...] = mine
    theirs_out[...] = theirs


def absorb(where, adj_rows, borrowed, slabs, sums, step, chunk, chunks, n_row):
    sections = len(slabs)
    rows = adj_rows.shape[0]
    deep, width = slabs[0].shape

    def own(s):
        return pl.BlockSpec(
            (rows, deep),
            lambda g, where: (
                0,
                (s * n_row + where[1 + step * sections + s] * CORES + where[0]) * chunks + chunk,
            ),
        )

    def other(s):
        return pl.BlockSpec(
            (rows, deep),
            lambda g, where: (0, s * chunks + chunk),
        )

    whole = lambda shape: pl.BlockSpec(shape, lambda g, where: (0, 0))
    shapes = [(rows, width), (rows + ONES, width)]
    first = sums is None
    operands = [adj_rows] * sections + [borrowed] * sections + list(slabs)
    in_specs = [own(s) for s in range(sections)] + [other(s) for s in range(sections)]
    in_specs += [whole((deep, width))] * sections
    if not first:
        operands += list(sums)
        in_specs += [whole(shape) for shape in shapes]
    at = 1 + 3 * sections
    return pl.pallas_call(
        functools.partial(absorb_kernel, sections, rows, first),
        grid_spec=pltpu.PrefetchScalarGridSpec(
            num_scalar_prefetch=1,
            grid=(1,),
            in_specs=in_specs,
            out_specs=[whole(shape) for shape in shapes],
        ),
        out_shape=[jax.ShapeDtypeStruct(shape, jnp.float32) for shape in shapes],
        input_output_aliases={} if first else {at: 0, at + 1: 1},
        compiler_params=pltpu.CompilerParams(vmem_limit_bytes=VMEM_LIMIT),
        cost_estimate=SHORT,
        name="absorb",
    )(where, *operands)


def make_shards(n_row):
    chips = n_row // CORES
    cycle = chip_cycle(chips)
    place = {chip: k for k, chip in enumerate(cycle)}

    def way(section):
        return 1 if section % 2 == 0 else -1

    def ring(step):
        return [
            (cycle[k] * CORES + c, cycle[(k + step) % chips] * CORES + c)
            for k in range(chips)
            for c in range(CORES)
        ]

    swap = [(d, d ^ 1) for d in range(n_row)]

    def shards(adj_rows, adj_panel, adj_tile):
        rows = adj_rows.shape[0]
        sections, depth, width = adj_panel.shape
        chunks = 2 if depth % 256 == 0 else 1
        deep = depth // chunks
        table = np.array(
            [
                [d % CORES]
                + [
                    cycle[(place[d // CORES] - way(s) * step) % chips]
                    for step in range(chips)
                    for s in range(sections)
                ]
                for d in range(n_row)
            ],
            np.int32,
        )
        where = jnp.asarray(table)[lax.axis_index("row")]

        held = [
            [adj_panel[s, j * deep : (j + 1) * deep] for s in range(sections)] for j in range(chunks)
        ]
        sums = None
        degree = []
        borrowed = {}
        due = [(0, j, held[j]) for j in range(chunks)]
        lends = list(range(chips))
        stretch = adj_rows.shape[1] // DEGREE_PARTS
        done = ()

        def tie(values, others):
            return lax.optimization_barrier((values, others))[0]

        for step in range(1, chips + 1):
            arrived = []
            for j in range(chunks):
                if step > 1:
                    held[j] = tie(held[j], done)
                if step < chips:
                    arrived.append([lax.ppermute(held[j][s], "row", ring(way(s))) for s in range(sections)])
                if step == 1:
                    continue
                now = tie(adj_rows, held[j])
                done = []
                at = step - 1
                while lends and lends[0] <= at + 1 and len(done) < MOST:
                    coming = lends.pop(0)
                    lent = lend(where, held[j][0], adj_rows, coming, sections, n_row, depth)
                    borrowed[coming] = lax.ppermute(lent, "row", swap)
                    done.append(lent)
                due.append((at, j, held[j]))
                if at > 1 or chips == 2:
                    for _ in range(MOST if step < chips else len(due)):
                        if due:
                            t, part, slabs = due.pop(0)
                            sums = absorb(
                                where, now, borrowed[t], tie(slabs, held[j]), sums, t, part, chunks, n_row
                            )
                            done.append(sums)
                if at > 2 and j == 0 and len(degree) < DEGREE_PARTS:
                    k = len(degree) * stretch
                    part = lax.slice_in_dim(now, k, k + stretch, axis=1)
                    degree.append(jnp.sum(part, axis=1, dtype=jnp.float32))
                    done.append(degree[-1])
            held = arrived
        degree = sum(degree)

        mine, theirs = sums
        partner = lax.ppermute(theirs, "row", swap)
        square = mine + partner[:rows]
        col_degree = theirs[rows : rows + 1] + partner[rows : rows + 1]
        tile = adj_tile.astype(jnp.float32)
        lower = jnp.minimum(degree[:, None], col_degree)
        intersection = (square + tile) / (lower + 1.0 - tile)
        return (intersection, degree)

    return shards


def solution(mesh):
    in_specs = (
        P(("parts", "row"), None),
        P(None, ("parts", "row"), None),
        P(("parts", "row"), None),
    )
    out_specs = (P(("parts", "row"), None), P(("parts", "row")))
    return jax.shard_map(
        make_shards(mesh.shape["row"]), mesh=mesh, in_specs=in_specs, out_specs=out_specs, check_vma=False
    )
```

```python
import functools

import jax
import jax.numpy as jnp
import numpy as np
from jax import lax
from jax.experimental import pallas as pl
from jax.experimental.pallas import tpu as pltpu
from jax.sharding import PartitionSpec as P

CORES = 2
ONES = 16
MOST = 2
DEGREE_PARTS = 2
SHORT = pl.CostEstimate(flops=0, bytes_accessed=1024, transcendentals=0)
VMEM_LIMIT = 24 * 1024 * 1024
LEND_LIMIT = 52 * 1024 * 1024


def chip_cycle(chips):
    wide = 1
    while (2 * wide) ** 2 <= chips:
        wide *= 2
    high = chips // wide
    if wide == 1 or high % 2 or wide * high != chips:
        return list(range(chips))
    walk = [(0, 0)]
    for i in range(high):
        line = range(1, wide)
        walk += [(i, j) for j in (line if i % 2 == 0 else reversed(line))]
    walk += [(i, 0) for i in range(high - 1, 0, -1)]
    return [i * wide + j for i, j in walk]


def lend_kernel(step, sections, n_row, depth, where, gate, rows_ref, own_ref, lent_ref, sems):
    copies = []
    for s in range(sections):
        pair = (s * n_row + where[1 + step * sections + s] * CORES) * depth
        for k, (ref, core) in enumerate(((own_ref, where[0]), (lent_ref, 1 - where[0]))):
            start = pl.multiple_of(pair + core * depth, 128)
            copies.append(
                pltpu.make_async_copy(
                    rows_ref.at[:, pl.ds(start, depth)],
                    ref.at[:, pl.ds(s * depth, depth)],
                    sems.at[s, k],
                )
            )
    for copy in copies:
        copy.start()
    for copy in copies:
        copy.wait()


def lend(where, gate, adj_rows, step, sections, n_row, depth):
    rows = adj_rows.shape[0]
    shape = jax.ShapeDtypeStruct((rows, sections * depth), adj_rows.dtype)
    return pl.pallas_call(
        functools.partial(lend_kernel, step, sections, n_row, depth),
        in_specs=[
            pl.BlockSpec(memory_space=pltpu.SMEM),
            pl.BlockSpec(memory_space=pl.ANY),
            pl.BlockSpec(memory_space=pltpu.HBM),
        ],
        out_specs=[pl.BlockSpec(memory_space=pltpu.VMEM)] * 2,
        out_shape=[shape, shape],
        scratch_shapes=[pltpu.SemaphoreType.DMA((sections, 2))],
        compiler_params=pltpu.CompilerParams(vmem_limit_bytes=LEND_LIMIT),
        cost_estimate=SHORT,
        name="lend",
    )(where, gate, adj_rows)


def absorb_kernel(sections, rows, first, *refs):
    own, other, slab = (refs[k * sections : (k + 1) * sections] for k in range(3))
    mine_out, theirs_out = refs[-2:]
    total = None
    for s in range(sections):
        ones = jnp.ones((ONES, own[s].shape[1]), own[s].dtype)
        left = jnp.concatenate([own[s][...], other[s][...], ones], axis=0)
        product = jnp.dot(left, slab[s][...], preferred_element_type=jnp.float32)
        total = product if total is None else total + product
    mine, theirs = total[:rows], total[rows:]
    if not first:
        mine_in, theirs_in = refs[3 * sections : 3 * sections + 2]
        mine, theirs = mine + mine_in[...], theirs + theirs_in[...]
    mine_out[...] = mine
    theirs_out[...] = theirs


def absorb(own, borrowed, slabs, sums, chunk, chunks):
    sections = len(slabs)
    rows = own.shape[0]
    deep, width = slabs[0].shape

    def block(s):
        return pl.BlockSpec((rows, deep), lambda g: (0, s * chunks + chunk))

    def whole(shape):
        return pl.BlockSpec(shape, lambda g: (0, 0))

    shapes = [(rows, width), (rows + ONES, width)]
    first = sums is None
    operands = [own] * sections + [borrowed] * sections + list(slabs)
    in_specs = [block(s) for s in range(sections)] * 2 + [whole((deep, width))] * sections
    if not first:
        operands += list(sums)
        in_specs += [whole(shape) for shape in shapes]
    at = 3 * sections
    return pl.pallas_call(
        functools.partial(absorb_kernel, sections, rows, first),
        grid=(1,),
        in_specs=in_specs,
        out_specs=[whole(shape) for shape in shapes],
        out_shape=[jax.ShapeDtypeStruct(shape, jnp.float32) for shape in shapes],
        input_output_aliases={} if first else {at: 0, at + 1: 1},
        compiler_params=pltpu.CompilerParams(vmem_limit_bytes=VMEM_LIMIT),
        cost_estimate=SHORT,
        name="absorb",
    )(*operands)


def make_shards(n_row):
    chips = n_row // CORES
    cycle = chip_cycle(chips)
    place = {chip: k for k, chip in enumerate(cycle)}

    def way(section):
        return 1 if section % 2 == 0 else -1

    def ring(step):
        return [
            (cycle[k] * CORES + c, cycle[(k + step) % chips] * CORES + c)
            for k in range(chips)
            for c in range(CORES)
        ]

    swap = [(d, d ^ 1) for d in range(n_row)]

    def shards(adj_rows, adj_panel, adj_tile):
        rows = adj_rows.shape[0]
        sections, depth, width = adj_panel.shape
        chunks = 2 if depth % 256 == 0 else 1
        deep = depth // chunks
        table = np.array(
            [
                [d % CORES]
                + [
                    cycle[(place[d // CORES] - way(s) * step) % chips]
                    for step in range(chips)
                    for s in range(sections)
                ]
                for d in range(n_row)
            ],
            np.int32,
        )
        where = jnp.asarray(table)[lax.axis_index("row")]

        held = [
            [adj_panel[s, j * deep : (j + 1) * deep] for s in range(sections)] for j in range(chunks)
        ]
        sums = None
        degree = []
        own = {}
        borrowed = {}
        due = [(0, j, held[j]) for j in range(chunks)]
        lends = list(range(chips))
        stretch = adj_rows.shape[1] // DEGREE_PARTS
        done = ()

        def tie(values, others):
            return lax.optimization_barrier((values, others))[0]

        for step in range(1, chips + 1):
            arrived = []
            for j in range(chunks):
                if step > 1:
                    held[j] = tie(held[j], done)
                if step < chips:
                    arrived.append([lax.ppermute(held[j][s], "row", ring(way(s))) for s in range(sections)])
                if step == 1:
                    continue
                now = tie(adj_rows, held[j])
                done = []
                at = step - 1
                while lends and lends[0] <= at + 1 and len(done) < MOST:
                    coming = lends.pop(0)
                    own[coming], lent = lend(where, held[j][0], adj_rows, coming, sections, n_row, depth)
                    borrowed[coming] = lax.ppermute(lent, "row", swap)
                    done.append(lent)
                due.append((at, j, held[j]))
                if at > 1 or chips == 2:
                    for _ in range(MOST if step < chips else len(due)):
                        if due:
                            t, part, slabs = due.pop(0)
                            sums = absorb(own[t], borrowed[t], tie(slabs, held[j]), sums, part, chunks)
                            done.append(sums)
                if at > 2 and j == 0 and len(degree) < DEGREE_PARTS:
                    k = len(degree) * stretch
                    part = lax.slice_in_dim(now, k, k + stretch, axis=1)
                    degree.append(jnp.sum(part, axis=1, dtype=jnp.float32))
                    done.append(degree[-1])
            held = arrived
        degree = sum(degree)

        mine, theirs = sums
        partner = lax.ppermute(theirs, "row", swap)
        square = mine + partner[:rows]
        col_degree = theirs[rows : rows + 1] + partner[rows : rows + 1]
        tile = adj_tile.astype(jnp.float32)
        lower = jnp.minimum(degree[:, None], col_degree)
        intersection = (square + tile) / (lower + 1.0 - tile)
        return (intersection, degree)

    return shards


def solution(mesh):
    in_specs = (
        P(("parts", "row"), None),
        P(None, ("parts", "row"), None),
        P(("parts", "row"), None),
    )
    out_specs = (P(("parts", "row"), None), P(("parts", "row")))
    return jax.shard_map(
        make_shards(mesh.shape["row"]), mesh=mesh, in_specs=in_specs, out_specs=out_specs, check_vma=False
    )
```

```python
import functools

import jax
import jax.numpy as jnp
import numpy as np
from jax import lax
from jax.experimental import pallas as pl
from jax.experimental.pallas import tpu as pltpu
from jax.sharding import PartitionSpec as P

CORES = 2
ONES = 16
MOST = 3
LENT = 4
LEND_AT = 2
ABSORB_FROM = 4
DEGREE_PARTS = 2
SHORT = pl.CostEstimate(flops=0, bytes_accessed=1024, transcendentals=0)
VMEM_LIMIT = 24 * 1024 * 1024
LEND_LIMIT = 52 * 1024 * 1024


def chip_cycle(chips):
    wide = 1
    while (2 * wide) ** 2 <= chips:
        wide *= 2
    high = chips // wide
    if wide == 1 or high % 2 or wide * high != chips:
        return list(range(chips))
    walk = [(0, 0)]
    for i in range(high):
        line = range(1, wide)
        walk += [(i, j) for j in (line if i % 2 == 0 else reversed(line))]
    walk += [(i, 0) for i in range(high - 1, 0, -1)]
    return [i * wide + j for i, j in walk]


def lend_kernel(sections, n_row, depth, where, gate, rows_ref, *refs):
    sems = refs[-1]
    per = refs[0].shape[1] // depth
    copies = []
    for k in range(per * (len(refs) - 1)):
        start = (k % sections * n_row + where[1 + k] * CORES + 1 - where[0]) * depth
        copies.append(
            pltpu.make_async_copy(
                rows_ref.at[:, pl.ds(pl.multiple_of(start, 128), depth)],
                refs[k // per].at[:, pl.ds(k % per * depth, depth)],
                sems.at[k],
            )
        )
    for copy in copies:
        copy.start()
    for copy in copies:
        copy.wait()


def lend(where, gate, adj_rows, sections, n_row, depth):
    blocks = sections * n_row // CORES
    shape = jax.ShapeDtypeStruct((adj_rows.shape[0], blocks // LENT * depth), adj_rows.dtype)
    return pl.pallas_call(
        functools.partial(lend_kernel, sections, n_row, depth),
        in_specs=[
            pl.BlockSpec(memory_space=pltpu.SMEM),
            pl.BlockSpec(memory_space=pl.ANY),
            pl.BlockSpec(memory_space=pl.ANY),
        ],
        out_specs=[pl.BlockSpec(memory_space=pl.ANY)] * LENT,
        out_shape=[shape] * LENT,
        scratch_shapes=[pltpu.SemaphoreType.DMA((blocks,))],
        compiler_params=pltpu.CompilerParams(vmem_limit_bytes=LEND_LIMIT),
        cost_estimate=SHORT,
        name="lend",
    )(where, gate, adj_rows)


def absorb_kernel(sections, rows, first, where, *refs):
    own, other, slab = (refs[k * sections : (k + 1) * sections] for k in range(3))
    mine_out, theirs_out = refs[-2:]
    total = None
    for s in range(sections):
        ones = jnp.ones((ONES, own[s].shape[1]), own[s].dtype)
        left = jnp.concatenate([own[s][...], other[s][...], ones], axis=0)
        product = jnp.dot(left, slab[s][...], preferred_element_type=jnp.float32)
        total = product if total is None else total + product
    mine, theirs = total[:rows], total[rows:]
    if not first:
        mine_in, theirs_in = refs[3 * sections : 3 * sections + 2]
        mine, theirs = mine + mine_in[...], theirs + theirs_in[...]
    mine_out[...] = mine
    theirs_out[...] = theirs


def absorb(where, adj_rows, borrowed, slabs, sums, step, chunk, chunks, n_row):
    sections = len(slabs)
    rows = adj_rows.shape[0]
    deep, width = slabs[0].shape

    def own(s):
        return pl.BlockSpec(
            (rows, deep),
            lambda g, where: (
                0,
                (s * n_row + where[1 + step * sections + s] * CORES + where[0]) * chunks + chunk,
            ),
        )

    per = n_row // CORES // LENT

    def other(s):
        return pl.BlockSpec((rows, deep), lambda g, where: (0, (step % per * sections + s) * chunks + chunk))

    def whole(shape):
        return pl.BlockSpec(shape, lambda g, where: (0, 0))

    shapes = [(rows, width), (rows + ONES, width)]
    first = sums is None
    operands = [adj_rows] * sections + [borrowed[step // per]] * sections + list(slabs)
    in_specs = [own(s) for s in range(sections)] + [other(s) for s in range(sections)]
    in_specs += [whole((deep, width))] * sections
    if not first:
        operands += list(sums)
        in_specs += [whole(shape) for shape in shapes]
    at = 1 + 3 * sections
    return pl.pallas_call(
        functools.partial(absorb_kernel, sections, rows, first),
        grid_spec=pltpu.PrefetchScalarGridSpec(
            num_scalar_prefetch=1,
            grid=(1,),
            in_specs=in_specs,
            out_specs=[whole(shape) for shape in shapes],
        ),
        out_shape=[jax.ShapeDtypeStruct(shape, jnp.float32) for shape in shapes],
        input_output_aliases={} if first else {at: 0, at + 1: 1},
        compiler_params=pltpu.CompilerParams(vmem_limit_bytes=VMEM_LIMIT),
        cost_estimate=SHORT,
        name="absorb",
    )(where, *operands)


def make_shards(n_row):
    chips = n_row // CORES
    cycle = chip_cycle(chips)
    place = {chip: k for k, chip in enumerate(cycle)}

    def way(section):
        return 1 if section % 2 == 0 else -1

    def ring(step):
        return [
            (cycle[k] * CORES + c, cycle[(k + step) % chips] * CORES + c)
            for k in range(chips)
            for c in range(CORES)
        ]

    swap = [(d, d ^ 1) for d in range(n_row)]

    def shards(adj_rows, adj_panel, adj_tile):
        rows = adj_rows.shape[0]
        sections, depth, width = adj_panel.shape
        chunks = 2 if depth % 256 == 0 else 1
        deep = depth // chunks
        table = np.array(
            [
                [d % CORES]
                + [
                    cycle[(place[d // CORES] - way(s) * step) % chips]
                    for step in range(chips)
                    for s in range(sections)
                ]
                for d in range(n_row)
            ],
            np.int32,
        )
        where = jnp.asarray(table)[lax.axis_index("row")]

        held = [
            [adj_panel[s, j * deep : (j + 1) * deep] for s in range(sections)] for j in range(chunks)
        ]
        sums = None
        degree = []
        due = [(0, j, held[j]) for j in range(chunks)]
        stretch = adj_rows.shape[1] // DEGREE_PARTS
        done = ()

        def tie(values, others):
            return lax.optimization_barrier((values, others))[0]

        for step in range(1, chips + 1):
            arrived = []
            for j in range(chunks):
                if step > 1:
                    held[j] = tie(held[j], done)
                if step < chips:
                    arrived.append([lax.ppermute(held[j][s], "row", ring(way(s))) for s in range(sections)])
                if step == 1:
                    continue
                at = step - 1
                done = []
                due.append((at, j, held[j]))
                if at == LEND_AT and j == chunks - 1:
                    lent = lend(where, held[j][0], adj_rows, sections, n_row, depth)
                    borrowed = [lax.ppermute(part, "row", swap) for part in lent]
                    done.append(lent)
                if at >= ABSORB_FROM:
                    now = tie(adj_rows, held[j])
                    for _ in range(MOST if step < chips else len(due)):
                        if due:
                            t, part, slabs = due.pop(0)
                            slabs = tie(slabs, held[j])
                            sums = absorb(where, now, borrowed, slabs, sums, t, part, chunks, n_row)
                            done.append(sums)
                    if at > ABSORB_FROM and j == 0 and len(degree) < DEGREE_PARTS:
                        k = len(degree) * stretch
                        part = lax.slice_in_dim(now, k, k + stretch, axis=1)
                        degree.append(jnp.sum(part, axis=1, dtype=jnp.float32))
                        done.append(degree[-1])
            held = arrived
        degree = sum(degree)

        mine, theirs = sums
        partner = lax.ppermute(theirs, "row", swap)
        square = mine + partner[:rows]
        col_degree = theirs[rows : rows + 1] + partner[rows : rows + 1]
        tile = adj_tile.astype(jnp.float32)
        lower = jnp.minimum(degree[:, None], col_degree)
        intersection = (square + tile) / (lower + 1.0 - tile)
        return (intersection, degree)

    return shards


def solution(mesh):
    in_specs = (
        P(("parts", "row"), None),
        P(None, ("parts", "row"), None),
        P(("parts", "row"), None),
    )
    out_specs = (P(("parts", "row"), None), P(("parts", "row")))
    return jax.shard_map(
        make_shards(mesh.shape["row"]), mesh=mesh, in_specs=in_specs, out_specs=out_specs, check_vma=False
    )
```

```python
import functools

import jax
import jax.numpy as jnp
import numpy as np
from jax import lax
from jax.experimental import pallas as pl
from jax.experimental.pallas import tpu as pltpu
from jax.sharding import PartitionSpec as P

CORES = 2
ONES = 16
SLOTS = 1
LENDS = 2
MOST = 3
LEND_FROM = 1
ABSORB_FROM = 2
DEGREE_PARTS = 2
SHORT = pl.CostEstimate(flops=0, bytes_accessed=1024, transcendentals=0)
VMEM_LIMIT = 24 * 1024 * 1024
LEND_LIMIT = 48 * 1024 * 1024


def chip_cycle(chips):
    wide = 1
    while (2 * wide) ** 2 <= chips:
        wide *= 2
    high = chips // wide
    if wide == 1 or high % 2 or wide * high != chips:
        return list(range(chips))
    walk = [(0, 0)]
    for i in range(high):
        line = range(1, wide)
        walk += [(i, j) for j in (line if i % 2 == 0 else reversed(line))]
    walk += [(i, 0) for i in range(high - 1, 0, -1)]
    return [i * wide + j for i, j in walk]


def lend_kernel(step, sections, n_row, depth, where, gate, rows_ref, own_ref, lent_ref, sems):
    copies = []
    for s in range(sections):
        pair = (s * n_row + where[1 + step * sections + s] * CORES) * depth
        for k, (ref, core) in enumerate(((own_ref, where[0]), (lent_ref, 1 - where[0]))):
            start = pl.multiple_of(pair + core * depth, 128)
            copies.append(
                pltpu.make_async_copy(
                    rows_ref.at[:, pl.ds(start, depth)],
                    ref.at[:, pl.ds(s * depth, depth)],
                    sems.at[s, k],
                )
            )
    for copy in copies:
        copy.start()
    for copy in copies:
        copy.wait()


def lend(where, gate, adj_rows, step, sections, n_row, depth):
    rows = adj_rows.shape[0]
    shape = jax.ShapeDtypeStruct((rows, sections * depth), adj_rows.dtype)
    return pl.pallas_call(
        functools.partial(lend_kernel, step, sections, n_row, depth),
        in_specs=[
            pl.BlockSpec(memory_space=pltpu.SMEM),
            pl.BlockSpec(memory_space=pl.ANY),
            pl.BlockSpec(memory_space=pltpu.HBM),
        ],
        out_specs=[pl.BlockSpec(memory_space=pltpu.VMEM)] * 2,
        out_shape=[shape, shape],
        scratch_shapes=[pltpu.SemaphoreType.DMA((sections, 2))],
        compiler_params=pltpu.CompilerParams(vmem_limit_bytes=LEND_LIMIT),
        cost_estimate=SHORT,
        name="lend",
    )(where, gate, adj_rows)


def absorb_kernel(sections, rows, first, *refs):
    own, other, slab = (refs[k * sections : (k + 1) * sections] for k in range(3))
    mine_out, theirs_out = refs[-2:]
    total = None
    for s in range(sections):
        ones = jnp.ones((ONES, own[s].shape[1]), own[s].dtype)
        left = jnp.concatenate([own[s][...], other[s][...], ones], axis=0)
        product = jnp.dot(left, slab[s][...], preferred_element_type=jnp.float32)
        total = product if total is None else total + product
    mine, theirs = total[:rows], total[rows:]
    if not first:
        mine_in, theirs_in = refs[3 * sections : 3 * sections + 2]
        mine, theirs = mine + mine_in[...], theirs + theirs_in[...]
    mine_out[...] = mine
    theirs_out[...] = theirs


def absorb(own, borrowed, slabs, sums, chunk, chunks):
    sections = len(slabs)
    rows = own.shape[0]
    deep, width = slabs[0].shape

    def block(s):
        return pl.BlockSpec((rows, deep), lambda g: (0, s * chunks + chunk))

    def whole(shape):
        return pl.BlockSpec(shape, lambda g: (0, 0))

    shapes = [(rows, width), (rows + ONES, width)]
    first = sums is None
    operands = [own] * sections + [borrowed] * sections + list(slabs)
    in_specs = [block(s) for s in range(sections)] * 2 + [whole((deep, width))] * sections
    if not first:
        operands += list(sums)
        in_specs += [whole(shape) for shape in shapes]
    at = 3 * sections
    return pl.pallas_call(
        functools.partial(absorb_kernel, sections, rows, first),
        grid=(1,),
        in_specs=in_specs,
        out_specs=[whole(shape) for shape in shapes],
        out_shape=[jax.ShapeDtypeStruct(shape, jnp.float32) for shape in shapes],
        input_output_aliases={} if first else {at: 0, at + 1: 1},
        compiler_params=pltpu.CompilerParams(vmem_limit_bytes=VMEM_LIMIT),
        cost_estimate=SHORT,
        name="absorb",
    )(*operands)


def make_shards(n_row):
    chips = n_row // CORES
    cycle = chip_cycle(chips)
    place = {chip: k for k, chip in enumerate(cycle)}

    def way(section):
        return 1 if section % 2 == 0 else -1

    def ring(step):
        return [
            (cycle[k] * CORES + c, cycle[(k + step) % chips] * CORES + c)
            for k in range(chips)
            for c in range(CORES)
        ]

    swap = [(d, d ^ 1) for d in range(n_row)]

    def shards(adj_rows, adj_panel, adj_tile):
        rows = adj_rows.shape[0]
        sections, depth, width = adj_panel.shape
        chunks = 1
        deep = depth // chunks
        table = np.array(
            [
                [d % CORES]
                + [
                    cycle[(place[d // CORES] - way(s) * step) % chips]
                    for step in range(chips)
                    for s in range(sections)
                ]
                for d in range(n_row)
            ],
            np.int32,
        )
        where = jnp.asarray(table)[lax.axis_index("row")]

        held = [
            [adj_panel[s, j * deep : (j + 1) * deep] for s in range(sections)] for j in range(chunks)
        ]
        sums = None
        degree = []
        own = {}
        borrowed = {}
        due = [(0, j, held[j]) for j in range(chunks)]
        lends = list(range(chips))
        stretch = adj_rows.shape[1] // DEGREE_PARTS
        past = []

        def tie(values, others):
            return lax.optimization_barrier((values, others))[0]

        for step in range(1, chips + 1):
            arrived = []
            for j in range(chunks):
                if step > 1:
                    held[j] = tie(held[j], past[-SLOTS] if len(past) >= SLOTS else ())
                if step < chips:
                    arrived.append([lax.ppermute(held[j][s], "row", ring(way(s))) for s in range(sections)])
                if step == 1:
                    continue
                now = tie(adj_rows, held[j])
                done = []
                past.append(done)
                at = step - 1
                while at >= LEND_FROM and lends and lends[0] <= at + 1 and len(done) < LENDS:
                    coming = lends.pop(0)
                    own[coming], lent = lend(where, held[j][0], adj_rows, coming, sections, n_row, depth)
                    borrowed[coming] = lax.ppermute(lent, "row", swap)
                    done.append(lent)
                due.append((at, j, held[j]))
                if at >= ABSORB_FROM:
                    for _ in range(MOST if step < chips else len(due)):
                        if due:
                            t, part, slabs = due.pop(0)
                            sums = absorb(own[t], borrowed[t], tie(slabs, held[j]), sums, part, chunks)
                            done.append(sums)
                if at > ABSORB_FROM and j == 0 and len(degree) < DEGREE_PARTS:
                    k = len(degree) * stretch
                    part = lax.slice_in_dim(now, k, k + stretch, axis=1)
                    degree.append(jnp.sum(part, axis=1, dtype=jnp.float32))
                    done.append(degree[-1])
            held = arrived
        degree = sum(degree)

        mine, theirs = sums
        partner = lax.ppermute(theirs, "row", swap)
        square = mine + partner[:rows]
        col_degree = theirs[rows : rows + 1] + partner[rows : rows + 1]
        tile = adj_tile.astype(jnp.float32)
        lower = jnp.minimum(degree[:, None], col_degree)
        intersection = (square + tile) / (lower + 1.0 - tile)
        return (intersection, degree)

    return shards


def solution(mesh):
    in_specs = (
        P(("parts", "row"), None),
        P(None, ("parts", "row"), None),
        P(("parts", "row"), None),
    )
    out_specs = (P(("parts", "row"), None), P(("parts", "row")))
    return jax.shard_map(
        make_shards(mesh.shape["row"]), mesh=mesh, in_specs=in_specs, out_specs=out_specs, check_vma=False
    )
```

```python
import functools

import jax
import jax.numpy as jnp
import numpy as np
from jax import lax
from jax.experimental import pallas as pl
from jax.experimental.pallas import tpu as pltpu
from jax.sharding import PartitionSpec as P

CORES = 2
ONES = 16
SLOTS = 3
LENDS = 2
MOST = 3
LEND_FROM = 1
ABSORB_FROM = 2
DEGREE_PARTS = 2
SHORT = pl.CostEstimate(flops=0, bytes_accessed=1024, transcendentals=0)
VMEM_LIMIT = 24 * 1024 * 1024
LEND_LIMIT = 48 * 1024 * 1024


def chip_cycle(chips):
    wide = 1
    while (2 * wide) ** 2 <= chips:
        wide *= 2
    high = chips // wide
    if wide == 1 or high % 2 or wide * high != chips:
        return list(range(chips))
    walk = [(0, 0)]
    for i in range(high):
        line = range(1, wide)
        walk += [(i, j) for j in (line if i % 2 == 0 else reversed(line))]
    walk += [(i, 0) for i in range(high - 1, 0, -1)]
    return [i * wide + j for i, j in walk]


def lend_kernel(step, sections, n_row, depth, where, gate, rows_ref, own_ref, lent_ref, sems):
    copies = []
    for s in range(sections):
        pair = (s * n_row + where[1 + step * sections + s] * CORES) * depth
        for k, (ref, core) in enumerate(((own_ref, where[0]), (lent_ref, 1 - where[0]))):
            start = pl.multiple_of(pair + core * depth, 128)
            copies.append(
                pltpu.make_async_copy(
                    rows_ref.at[:, pl.ds(start, depth)],
                    ref.at[:, pl.ds(s * depth, depth)],
                    sems.at[s, k],
                )
            )
    for copy in copies:
        copy.start()
    for copy in copies:
        copy.wait()


def lend(where, gate, adj_rows, step, sections, n_row, depth):
    rows = adj_rows.shape[0]
    shape = jax.ShapeDtypeStruct((rows, sections * depth), adj_rows.dtype)
    return pl.pallas_call(
        functools.partial(lend_kernel, step, sections, n_row, depth),
        in_specs=[
            pl.BlockSpec(memory_space=pltpu.SMEM),
            pl.BlockSpec(memory_space=pl.ANY),
            pl.BlockSpec(memory_space=pltpu.HBM),
        ],
        out_specs=[pl.BlockSpec(memory_space=pltpu.VMEM)] * 2,
        out_shape=[shape, shape],
        scratch_shapes=[pltpu.SemaphoreType.DMA((sections, 2))],
        compiler_params=pltpu.CompilerParams(vmem_limit_bytes=LEND_LIMIT),
        cost_estimate=SHORT,
        name="lend",
    )(where, gate, adj_rows)


def absorb_kernel(sections, rows, first, *refs):
    own, other, slab = (refs[k * sections : (k + 1) * sections] for k in range(3))
    mine_out, theirs_out = refs[-2:]
    total = None
    for s in range(sections):
        ones = jnp.ones((ONES, own[s].shape[1]), own[s].dtype)
        left = jnp.concatenate([own[s][...], other[s][...], ones], axis=0)
        product = jnp.dot(left, slab[s][...], preferred_element_type=jnp.float32)
        total = product if total is None else total + product
    mine, theirs = total[:rows], total[rows:]
    if not first:
        mine_in, theirs_in = refs[3 * sections : 3 * sections + 2]
        mine, theirs = mine + mine_in[...], theirs + theirs_in[...]
    mine_out[...] = mine
    theirs_out[...] = theirs


def absorb(own, borrowed, slabs, sums, chunk, chunks):
    sections = len(slabs)
    rows = own.shape[0]
    deep, width = slabs[0].shape

    def block(s):
        return pl.BlockSpec((rows, deep), lambda g: (0, s * chunks + chunk))

    def whole(shape):
        return pl.BlockSpec(shape, lambda g: (0, 0))

    shapes = [(rows, width), (rows + ONES, width)]
    first = sums is None
    operands = [own] * sections + [borrowed] * sections + list(slabs)
    in_specs = [block(s) for s in range(sections)] * 2 + [whole((deep, width))] * sections
    if not first:
        operands += list(sums)
        in_specs += [whole(shape) for shape in shapes]
    at = 3 * sections
    return pl.pallas_call(
        functools.partial(absorb_kernel, sections, rows, first),
        grid=(1,),
        in_specs=in_specs,
        out_specs=[whole(shape) for shape in shapes],
        out_shape=[jax.ShapeDtypeStruct(shape, jnp.float32) for shape in shapes],
        input_output_aliases={} if first else {at: 0, at + 1: 1},
        compiler_params=pltpu.CompilerParams(vmem_limit_bytes=VMEM_LIMIT),
        cost_estimate=SHORT,
        name="absorb",
    )(*operands)


def make_shards(n_row):
    chips = n_row // CORES
    cycle = chip_cycle(chips)
    place = {chip: k for k, chip in enumerate(cycle)}

    def way(section):
        return 1 if section % 2 == 0 else -1

    def ring(step):
        return [
            (cycle[k] * CORES + c, cycle[(k + step) % chips] * CORES + c)
            for k in range(chips)
            for c in range(CORES)
        ]

    swap = [(d, d ^ 1) for d in range(n_row)]

    def shards(adj_rows, adj_panel, adj_tile):
        rows = adj_rows.shape[0]
        sections, depth, width = adj_panel.shape
        chunks = 2 if depth % 256 == 0 else 1
        deep = depth // chunks
        table = np.array(
            [
                [d % CORES]
                + [
                    cycle[(place[d // CORES] - way(s) * step) % chips]
                    for step in range(chips)
                    for s in range(sections)
                ]
                for d in range(n_row)
            ],
            np.int32,
        )
        where = jnp.asarray(table)[lax.axis_index("row")]

        held = [
            [adj_panel[s, j * deep : (j + 1) * deep] for s in range(sections)] for j in range(chunks)
        ]
        sums = None
        degree = []
        own = {}
        borrowed = {}
        due = [(0, j, held[j]) for j in range(chunks)]
        lends = list(range(chips))
        stretch = adj_rows.shape[1] // DEGREE_PARTS
        past = []

        def tie(values, others):
            return lax.optimization_barrier((values, others))[0]

        for step in range(1, chips + 1):
            arrived = []
            for j in range(chunks):
                if step > 1:
                    held[j] = tie(held[j], past[-SLOTS] if len(past) >= SLOTS else ())
                if step < chips:
                    arrived.append([lax.ppermute(held[j][s], "row", ring(way(s))) for s in range(sections)])
                if step == 1:
                    continue
                now = tie(adj_rows, held[j])
                done = []
                past.append(done)
                at = step - 1
                while at >= LEND_FROM and lends and lends[0] <= at + 1 and len(done) < LENDS:
                    coming = lends.pop(0)
                    own[coming], lent = lend(where, held[j][0], adj_rows, coming, sections, n_row, depth)
                    borrowed[coming] = lax.ppermute(lent, "row", swap)
                    done.append(lent)
                due.append((at, j, held[j]))
                if at >= ABSORB_FROM:
                    for _ in range(MOST if step < chips else len(due)):
                        if due:
                            t, part, slabs = due.pop(0)
                            sums = absorb(own[t], borrowed[t], tie(slabs, held[j]), sums, part, chunks)
                            done.append(sums)
                if at > ABSORB_FROM and j == 0 and len(degree) < DEGREE_PARTS:
                    k = len(degree) * stretch
                    part = lax.slice_in_dim(now, k, k + stretch, axis=1)
                    degree.append(jnp.sum(part, axis=1, dtype=jnp.float32))
                    done.append(degree[-1])
            held = arrived
        degree = sum(degree)

        mine, theirs = sums
        partner = lax.ppermute(theirs, "row", swap)
        square = mine + partner[:rows]
        col_degree = theirs[rows : rows + 1] + partner[rows : rows + 1]
        tile = adj_tile.astype(jnp.float32)
        lower = jnp.minimum(degree[:, None], col_degree)
        intersection = (square + tile) / (lower + 1.0 - tile)
        return (intersection, degree)

    return shards


def solution(mesh):
    in_specs = (
        P(("parts", "row"), None),
        P(None, ("parts", "row"), None),
        P(("parts", "row"), None),
    )
    out_specs = (P(("parts", "row"), None), P(("parts", "row")))
    return jax.shard_map(
        make_shards(mesh.shape["row"]), mesh=mesh, in_specs=in_specs, out_specs=out_specs, check_vma=False
    )
```

```python
import functools

import jax
import jax.numpy as jnp
import numpy as np
from jax import lax
from jax.experimental import pallas as pl
from jax.experimental.pallas import tpu as pltpu
from jax.sharding import PartitionSpec as P

CORES = 2
ONES = 16
SHIPS = True
PER_LENT = 4
EARLY = 2
REST_AT = 3
MOST = 2
ABSORB_FROM = 2
DEGREE_PARTS = 8
DEGREE_AT = 3
HELP_AT = (3, 4)
TILE = 128
SHORT = pl.CostEstimate(flops=0, bytes_accessed=1024, transcendentals=0)
VMEM_LIMIT = 40 * 1024 * 1024
LEND_LIMIT = 44 * 1024 * 1024


def chip_cycle(chips):
    wide = 1
    while (2 * wide) ** 2 <= chips:
        wide *= 2
    high = chips // wide
    if wide == 1 or high % 2 or wide * high != chips:
        return list(range(chips))
    walk = [(0, 0)]
    for i in range(high):
        line = range(1, wide)
        walk += [(i, j) for j in (line if i % 2 == 0 else reversed(line))]
    walk += [(i, 0) for i in range(high - 1, 0, -1)]
    walk = walk[:1] + walk[:0:-1]
    return [i * wide + j for i, j in walk]


def make_rounds(chips, ships):
    if not ships:
        turns = [{"up": [("own", 0)] * 4, "down": [("own", 1)] * 4}]
        for r in range(1, chips - 1):
            turns.append({"up": [("up", r)] * 4, "down": [("down", r)] * 4})
        return turns
    up = [[("up", r)] * 4 for r in range(6)]
    down = [[("down", r)] * 4 for r in range(6)]
    up[0], down[0] = [("own", 0)] * 4, [("own", 1)] * 4
    up[1][3], down[1][0] = ("own", 1), ("own", 0)
    up[2][0], down[2][3] = ("ship", 0), ("ship", 0)
    up[3][0], down[3][3] = ("ship", 1), ("ship", 1)
    up[3][1], down[3][2] = ("ch", 2), ("ch", 2)
    up[4][1], down[4][2] = ("ch", 3), ("ch", 3)
    turns = [{"up": up[r], "down": down[r]} for r in range(6)]
    for r, inner in {
        1: (("own", 1), ("own", 0)),
        2: (("down", 1), ("up", 1)),
        3: (("up", 2), ("down", 2)),
        4: (("down", 4), ("up", 4)),
    }.items():
        turns[r]["ch"] = [inner[0], inner[0], inner[1], inner[1]]
    return turns


def make_routes(chips):
    return {
        "up": {p: (p + 1) % chips for p in range(chips)},
        "down": {p: (p - 1) % chips for p in range(chips)},
        "ch": {1: 6, 6: 1, 2: 5, 5: 2},
    }


def shipped(p, which):
    if p % 4 == 0:
        return ((p + 1) % 8 if which == 0 else (p + 6) % 8), 0
    return ((p - 1) % 8 if which == 0 else (p - 6) % 8), 1


def trace_blocks(chips, turns):
    routes = make_routes(chips)
    held = {("own", s): [(p, s) for p in range(chips)] for s in range(2)}
    held |= {("ship", k): [None] * chips for k in range(2)}
    for r, turn in enumerate(turns, 1):
        for port, sources in turn.items():
            held[port, r] = [None] * chips
            for p, q in routes[port].items():
                held[port, r][q] = held[sources[p % 4]][p]
    return held


def lend_kernel(starts, depth, where, rows_ref, *refs):
    sems = refs[-1]
    copies = []
    for k, slot in enumerate(starts):
        start = pl.multiple_of((where[slot] + 1 - where[0]) * depth, 128)
        copies.append(
            pltpu.make_async_copy(
                rows_ref.at[:, pl.ds(start, depth)],
                refs[k // PER_LENT].at[:, pl.ds(k % PER_LENT * depth, depth)],
                sems.at[k],
            )
        )
    for copy in copies:
        copy.start()
    for copy in copies:
        copy.wait()


def lend(where, adj_rows, starts, depth):
    rows = adj_rows.shape[0]
    parts = len(starts) // PER_LENT
    shape = jax.ShapeDtypeStruct((rows, PER_LENT * depth), adj_rows.dtype)
    return pl.pallas_call(
        functools.partial(lend_kernel, starts, depth),
        in_specs=[pl.BlockSpec(memory_space=pltpu.SMEM), pl.BlockSpec(memory_space=pl.ANY)],
        out_specs=[pl.BlockSpec(memory_space=pltpu.VMEM)] * parts,
        out_shape=[shape] * parts,
        scratch_shapes=[pltpu.SemaphoreType.DMA((len(starts),))],
        compiler_params=pltpu.CompilerParams(vmem_limit_bytes=LEND_LIMIT),
        cost_estimate=SHORT,
        name="lend",
    )(where, adj_rows)


def degree_kernel(core, first, where, rows_ref, *refs):
    out_ref = refs[-1]
    g = pl.program_id(0)

    @pl.when(g == 0)
    def _():
        out_ref[...] = jnp.zeros_like(out_ref) if first else refs[0][...]

    @pl.when(where[0] == core)
    def _():
        for k in range(rows_ref.shape[1] // 128):
            out_ref[...] += rows_ref[:, k * 128 : (k + 1) * 128].astype(jnp.float32)


def row_sums(where, adj_rows, core, sums):
    rows, columns = adj_rows.shape
    block = columns // DEGREE_PARTS
    lanes = pl.BlockSpec((rows, 128), lambda g, where: (0, 0))
    first = sums is None
    return pl.pallas_call(
        functools.partial(degree_kernel, core, first),
        grid_spec=pltpu.PrefetchScalarGridSpec(
            num_scalar_prefetch=1,
            grid=(DEGREE_PARTS,),
            in_specs=[
                pl.BlockSpec((rows, block), lambda g, where: (0, jnp.where(where[0] == core, g, 0))),
            ]
            + ([] if first else [lanes]),
            out_specs=lanes,
        ),
        out_shape=jax.ShapeDtypeStruct((rows, 128), jnp.float32),
        compiler_params=pltpu.CompilerParams(vmem_limit_bytes=LEND_LIMIT),
        cost_estimate=SHORT,
        name="degree",
    )(where, adj_rows, *([] if first else [sums]))


def absorb_kernel(count, flags, rows, first, where, *refs):
    own, other, slab = (refs[k * count : (k + 1) * count] for k in range(3))
    mine_out, theirs_out = refs[-2:]
    total = None
    for k in range(count):
        ones = jnp.ones((ONES, own[k].shape[1]), own[k].dtype)
        left = jnp.concatenate([own[k][...], other[k][...], ones], axis=0)
        product = jnp.dot(left, slab[k][...], preferred_element_type=jnp.float32)
        if flags[k] is not None:
            product = jnp.where(where[flags[k]] > 0, product, 0.0)
        total = product if total is None else total + product
    mine, theirs = total[:rows], total[rows:]
    if not first:
        mine_in, theirs_in = refs[3 * count : 3 * count + 2]
        mine, theirs = mine + mine_in[...], theirs + theirs_in[...]
    mine_out[...] = mine
    theirs_out[...] = theirs


def absorb(where, adj_rows, borrowed, slabs, slots, columns, flags, sums):
    count = len(slabs)
    rows = adj_rows.shape[0]
    depth, width = slabs[0].shape

    def own(k):
        return pl.BlockSpec((rows, depth), lambda g, where: (0, where[slots[k]] + where[0]))

    def other(k):
        return pl.BlockSpec((rows, depth), lambda g, where: (0, columns[k] % PER_LENT))

    def whole(shape):
        return pl.BlockSpec(shape, lambda g, where: (0, 0))

    shapes = [(rows, width), (rows + ONES, width)]
    first = sums is None
    operands = [adj_rows] * count + [borrowed[column // PER_LENT] for column in columns] + list(slabs)
    in_specs = [own(k) for k in range(count)] + [other(k) for k in range(count)]
    in_specs += [whole((depth, width))] * count
    if not first:
        operands += list(sums)
        in_specs += [whole(shape) for shape in shapes]
    at = 1 + 3 * count
    return pl.pallas_call(
        functools.partial(absorb_kernel, count, flags, rows, first),
        grid_spec=pltpu.PrefetchScalarGridSpec(
            num_scalar_prefetch=1,
            grid=(1,),
            in_specs=in_specs,
            out_specs=[whole(shape) for shape in shapes],
        ),
        out_shape=[jax.ShapeDtypeStruct(shape, jnp.float32) for shape in shapes],
        input_output_aliases={} if first else {at: 0, at + 1: 1},
        compiler_params=pltpu.CompilerParams(vmem_limit_bytes=VMEM_LIMIT),
        cost_estimate=SHORT,
        name="absorb",
    )(where, *operands)


def pick_kernel(choices, n_in, where, *refs):
    outs = refs[n_in:]
    for out, by_kind in zip(outs, choices):
        for source in sorted(set(by_kind), key=str):
            kinds = [kind for kind, chosen in enumerate(by_kind) if chosen == source]
            here = where[1] == kinds[0]
            for kind in kinds[1:]:
                here = here | (where[1] == kind)

            def send(out=out, source=source):
                if isinstance(source, int):
                    out[...] = refs[source][...]
                    return
                left = jnp.concatenate([refs[source[0]][...], refs[source[1]][...]], axis=0)
                for i in range(left.shape[0] // TILE):
                    for k in range(left.shape[1] // TILE):
                        out[k * TILE : (k + 1) * TILE, i * TILE : (i + 1) * TILE] = left[
                            i * TILE : (i + 1) * TILE, k * TILE : (k + 1) * TILE
                        ]

            pl.when(here)(send)


def pick(where, operands, specs, choices, shape):
    return pl.pallas_call(
        functools.partial(pick_kernel, choices, len(operands)),
        grid_spec=pltpu.PrefetchScalarGridSpec(
            num_scalar_prefetch=1,
            grid=(1,),
            in_specs=specs,
            out_specs=[pl.BlockSpec(shape.shape, lambda g, where: (0, 0))] * len(choices),
        ),
        out_shape=[shape] * len(choices),
        compiler_params=pltpu.CompilerParams(vmem_limit_bytes=VMEM_LIMIT),
        cost_estimate=SHORT,
        name="pick",
    )(where, *operands)


def help_kernel(rows, first, where, *refs):
    mine_out, theirs_out, left = refs[-3:]
    if first:
        mine_out[...] = jnp.zeros_like(mine_out)
        theirs_out[...] = jnp.zeros_like(theirs_out)
    else:
        mine_out[...] = refs[4][...]
        theirs_out[...] = refs[5][...]
    for kind in (1, 2):
        packed, slab = refs[kind - 1], refs[kind + 1]

        @pl.when(where[1] == kind)
        def _(packed=packed, slab=slab):
            depth, width = packed.shape
            for i in range(width // TILE):
                for k in range(depth // TILE):
                    left[i * TILE : (i + 1) * TILE, k * TILE : (k + 1) * TILE] = packed[
                        k * TILE : (k + 1) * TILE, i * TILE : (i + 1) * TILE
                    ]
            left[width:, :] = jnp.ones((ONES, depth), left.dtype)
            product = jnp.dot(left[...], slab[...], preferred_element_type=jnp.float32)
            mine_out[...] += product[:rows]
            theirs_out[...] += product[rows:]


def help_corner(where, up, down, slabs, rows, sums):
    depth, width = up.shape
    shapes = [(rows, width), (rows + ONES, width)]
    first = sums is None
    operands = [up, down, *slabs] + ([] if first else list(sums))

    def whole(shape):
        return pl.BlockSpec(shape, lambda g, where: (0, 0))

    return pl.pallas_call(
        functools.partial(help_kernel, rows, first),
        grid_spec=pltpu.PrefetchScalarGridSpec(
            num_scalar_prefetch=1,
            grid=(1,),
            in_specs=[whole((depth, width))] * 4 + ([] if first else [whole(s) for s in shapes]),
            out_specs=[whole(shape) for shape in shapes],
            scratch_shapes=[pltpu.VMEM((width + ONES, depth), up.dtype)],
        ),
        out_shape=[jax.ShapeDtypeStruct(shape, jnp.float32) for shape in shapes],
        compiler_params=pltpu.CompilerParams(vmem_limit_bytes=VMEM_LIMIT),
        cost_estimate=SHORT,
        name="help",
    )(where, *operands)


def make_shards(n_row):
    chips = n_row // CORES
    cycle = chip_cycle(chips)
    place = {chip: k for k, chip in enumerate(cycle)}
    routes = make_routes(chips)

    def pairs(route):
        return [(cycle[p] * CORES + c, cycle[q] * CORES + c) for p, q in route.items() for c in range(CORES)]

    swap = [(d, d ^ 1) for d in range(n_row)]

    def shards(adj_rows, adj_panel, adj_tile):
        rows = adj_rows.shape[0]
        sections, depth, width = adj_panel.shape
        ships = SHIPS and chips == 8 and 2 * rows == width and width % TILE == 0 and depth % TILE == 0
        turns = make_rounds(chips, ships)
        blocks = trace_blocks(chips, turns)
        rounds = len(turns)

        groups = [[("own", 0), ("own", 1)]] + [[(port, r) for port in turn] for r, turn in enumerate(turns, 1)]
        sources = [source for group in groups for source in group]
        if ships:
            sources = [("ship", 0), ("ship", 1)] + sources
        slots, flags, columns = {}, {}, {}
        table = [[d % CORES, place[d // CORES] % 4] for d in range(n_row)]
        for k, source in enumerate(sources):
            columns[source], slots[source] = k, 2 + 2 * k
            masked = source[0] in ("up", "down") and None in blocks[source]
            flags[source] = 3 + 2 * k if masked else None
            for d in range(n_row):
                p = place[d // CORES]
                block = blocks[source][p]
                if source[0] == "ship" and p % 4 in (0, 3):
                    block = shipped(p, source[1])
                owner, s = block or (p, 0)
                table[d] += [s * n_row + cycle[owner] * CORES, int(block is not None)]
        where = jnp.asarray(np.array(table, np.int32))[lax.axis_index("row")]

        def tie(values, others):
            return lax.optimization_barrier((values, others))[0]

        def depart(turn):
            sending, mixed = {}, {}
            for port, chosen in turn.items():
                if len(set(chosen)) == 1:
                    sending[port] = slab[chosen[0]]
                else:
                    mixed[port] = chosen
            if not mixed:
                return sending
            operands, specs, index = [], [], {}
            for source in sorted({source for chosen in mixed.values() for source in chosen}):
                if source[0] == "ship":
                    spec = pl.BlockSpec((rows, depth), lambda g, where, slot=slots[source]: (0, where[slot] + where[0]))
                    lent = pl.BlockSpec((rows, depth), lambda g, where, column=columns[source]: (0, column % PER_LENT))
                    index[source] = (len(operands), len(operands) + 1)
                    operands += [adj_rows, borrowed[columns[source] // PER_LENT]]
                    specs += [spec, lent]
                else:
                    index[source] = len(operands)
                    operands.append(slab[source])
                    specs.append(pl.BlockSpec((depth, width), lambda g, where: (0, 0)))
            choices = [[index[source] for source in chosen] for chosen in mixed.values()]
            shape = jax.ShapeDtypeStruct((depth, width), adj_panel.dtype)
            sending.update(zip(mixed, pick(where, operands, specs, choices, shape)))
            return sending

        slab = {("own", s): adj_panel[s] for s in range(sections)}
        lent = lend(where, tie(adj_rows, list(slab.values())), [slots[source] for source in sources], depth)
        borrowed = [lax.ppermute(part, "row", swap) for part in lent[:EARLY]]
        sums, helped = None, None
        due = [0]
        done = ()
        for r in range(1, rounds + 2):
            at = r - 1
            if at > 0:
                arrived = tie([slab[port, at] for port in turns[at - 1]], done)
                slab |= {(port, at): piece for port, piece in zip(turns[at - 1], arrived)}
                due.append(at)
            if at == 1:
                lanes = row_sums(where, tie(adj_rows, arrived), 1, None)
                arrived, lanes = lax.optimization_barrier((arrived, lanes))
                slab |= {(port, at): piece for port, piece in zip(turns[at - 1], arrived)}
            if r <= rounds:
                sending = depart(turns[r - 1])
                for port, piece in sending.items():
                    slab[port, r] = lax.ppermute(piece, "row", pairs(routes[port]))
                if r == REST_AT:
                    rest = tie(lent[EARLY:], list(sending.values()))
                    borrowed += [lax.ppermute(part, "row", swap) for part in rest]
            if at == 0:
                continue
            gate = arrived[0]
            now = tie(adj_rows, arrived)
            done = []
            if ships and at in HELP_AT:
                held = [slab["ch", 2]] * 2 if helped else [slab["own", 0], slab["own", 1]]
                helped = help_corner(where, slab["up", at], slab["down", at], tie(held, gate), rows, helped)
                done.append(helped)
            if at >= ABSORB_FROM:
                for _ in range(MOST if r <= rounds else len(due)):
                    if due:
                        t = due.pop(0)
                        slabs = tie([slab[source] for source in groups[t]], gate)
                        sums = absorb(
                            where,
                            now,
                            borrowed,
                            slabs,
                            [slots[source] for source in groups[t]],
                            [columns[source] for source in groups[t]],
                            [flags[source] for source in groups[t]],
                            sums,
                        )
                        done.append(sums)
            if at == DEGREE_AT:
                lanes = row_sums(where, now, 0, lanes)
                done.append(lanes)
        degree = jnp.sum(lanes, axis=1)

        mine, theirs = sums
        if ships:
            other = lax.ppermute(helped[1], "row", swap)
            joined = jnp.concatenate([helped[0] + other[:rows], helped[1][rows:] + other[rows:]], axis=0)
            returned = lax.ppermute(joined, "row", pairs({1: 0, 2: 3, 5: 4, 6: 7}))
        partner = lax.ppermute(theirs, "row", swap)
        square = mine + partner[:rows]
        col_degree = theirs[rows : rows + 1] + partner[rows : rows + 1]
        if ships:
            square = square + returned[:rows]
            col_degree = col_degree + returned[rows : rows + 1]
        tile = adj_tile.astype(jnp.float32)
        lower = jnp.minimum(degree[:, None], col_degree)
        intersection = (square + tile) / (lower + 1.0 - tile)
        return (intersection, degree)

    return shards


def solution(mesh):
    in_specs = (
        P(("parts", "row"), None),
        P(None, ("parts", "row"), None),
        P(("parts", "row"), None),
    )
    out_specs = (P(("parts", "row"), None), P(("parts", "row")))
    return jax.shard_map(
        make_shards(mesh.shape["row"]), mesh=mesh, in_specs=in_specs, out_specs=out_specs, check_vma=False
    )
```

```python
import functools

import jax
import jax.numpy as jnp
import numpy as np
from jax import lax
from jax.experimental import pallas as pl
from jax.experimental.pallas import tpu as pltpu
from jax.sharding import PartitionSpec as P

CORES = 2
ONES = 16
SHIPS = True
SLOTS = 1
MOST = 2
ABSORB_FROM = 3
PER_LENT = 4
EARLY = 1
REST_AT = 2
DEGREE_PARTS = 4
DEGREE_AT = 3
HELP_AT = (3, 4)
LEND_AFTER = 0
TILE = 128
SHORT = pl.CostEstimate(flops=0, bytes_accessed=1024, transcendentals=0)
VMEM_LIMIT = 40 * 1024 * 1024
LEND_LIMIT = 44 * 1024 * 1024


def chip_cycle(chips):
    wide = 1
    while (2 * wide) ** 2 <= chips:
        wide *= 2
    high = chips // wide
    if wide == 1 or high % 2 or wide * high != chips:
        return list(range(chips))
    walk = [(0, 0)]
    for i in range(high):
        line = range(1, wide)
        walk += [(i, j) for j in (line if i % 2 == 0 else reversed(line))]
    walk += [(i, 0) for i in range(high - 1, 0, -1)]
    walk = walk[:1] + walk[:0:-1]
    return [i * wide + j for i, j in walk]


def make_rounds(chips, ships):
    count = 6 if ships else chips - 1
    main = [[("own", 0)] * 4] + [[("main", r)] * 4 for r in range(1, count)]
    turns = [{"main": sources} for sources in main]
    if ships:
        main[1][3] = ("own", 1)
        main[2][0] = ("ship", 0)
        main[3][0] = ("ship", 1)
        main[3][1] = ("ch", 2)
        main[4][1] = ("ch", 3)
        for r, source in ((1, ("own", 0)), (2, ("main", 1)), (3, ("main", 2)), (4, ("main", 4))):
            turns[r]["ch"] = [source] * 4
    return turns


def make_route(chips, port, r):
    if port == "main":
        return {p: (p + 1) % chips for p in range(chips)}
    return {1: 6, 5: 2} if r == 4 else {6: 1, 2: 5}


def trace_blocks(chips, turns):
    held = {("own", s): [(p, s) for p in range(chips)] for s in range(2)}
    corner = [p % 4 == 0 for p in range(chips)]
    for k, ahead in enumerate((1, 6)):
        held["ship", k] = [((p + ahead) % chips, 0) if corner[p] else None for p in range(chips)]
    for r, turn in enumerate(turns, 1):
        for port, sources in turn.items():
            held[port, r] = [None] * chips
            for p, q in make_route(chips, port, r).items():
                source = sources[p % 4]
                held[port, r][q] = None if source[0] == "ship" else held[source][p]
    return held


def lend_kernel(sizes, first, depth, where, rows_ref, *refs):
    sems = refs[-1]
    copies = []
    for part, size in enumerate(sizes):
        for k in range(size):
            unit = sum(sizes[:part]) + k
            start = pl.multiple_of(where[first + unit] * depth, 128)
            copies.append(
                pltpu.make_async_copy(
                    rows_ref.at[:, pl.ds(start, depth)],
                    refs[part].at[:, pl.ds(k * depth, depth)],
                    sems.at[unit],
                )
            )
    for copy in copies:
        copy.start()
    for copy in copies:
        copy.wait()


def lend(where, adj_rows, sizes, first, depth):
    rows = adj_rows.shape[0]
    return pl.pallas_call(
        functools.partial(lend_kernel, sizes, first, depth),
        in_specs=[pl.BlockSpec(memory_space=pltpu.SMEM), pl.BlockSpec(memory_space=pl.ANY)],
        out_specs=[pl.BlockSpec(memory_space=pltpu.VMEM)] * len(sizes),
        out_shape=[jax.ShapeDtypeStruct((rows, size * depth), adj_rows.dtype) for size in sizes],
        scratch_shapes=[pltpu.SemaphoreType.DMA((sum(sizes),))],
        compiler_params=pltpu.CompilerParams(vmem_limit_bytes=LEND_LIMIT),
        cost_estimate=SHORT,
        name="lend",
    )(where, adj_rows)


def absorb_kernel(count, flags, rows, first, where, *refs):
    own, other, slab = (refs[k * count : (k + 1) * count] for k in range(3))
    mine_out, theirs_out = refs[-2:]
    total = None
    for k in range(count):
        ones = jnp.ones((ONES, own[k].shape[1]), own[k].dtype)
        left = jnp.concatenate([own[k][...], other[k][...], ones], axis=0)
        product = jnp.dot(left, slab[k][...], preferred_element_type=jnp.float32)
        if flags[k] is not None:
            product = jnp.where(where[flags[k]] > 0, product, 0.0)
        total = product if total is None else total + product
    mine, theirs = total[:rows], total[rows:]
    if not first:
        mine_in, theirs_in = refs[3 * count : 3 * count + 2]
        mine, theirs = mine + mine_in[...], theirs + theirs_in[...]
    mine_out[...] = mine
    theirs_out[...] = theirs


def absorb(where, adj_rows, borrowed, slabs, units, flags, sums):
    count = len(slabs)
    rows = adj_rows.shape[0]
    depth, width = slabs[0].shape

    def own(k):
        return pl.BlockSpec((rows, depth), lambda g, where: (0, where[2 + units[k]]))

    def other(k):
        return pl.BlockSpec((rows, depth), lambda g, where: (0, units[k] % PER_LENT))

    def whole(shape):
        return pl.BlockSpec(shape, lambda g, where: (0, 0))

    shapes = [(rows, width), (rows + ONES, width)]
    first = sums is None
    operands = [adj_rows] * count + [borrowed[unit // PER_LENT] for unit in units] + list(slabs)
    in_specs = [own(k) for k in range(count)] + [other(k) for k in range(count)]
    in_specs += [whole((depth, width))] * count
    if not first:
        operands += list(sums)
        in_specs += [whole(shape) for shape in shapes]
    at = 1 + 3 * count
    return pl.pallas_call(
        functools.partial(absorb_kernel, count, flags, rows, first),
        grid_spec=pltpu.PrefetchScalarGridSpec(
            num_scalar_prefetch=1,
            grid=(1,),
            in_specs=in_specs,
            out_specs=[whole(shape) for shape in shapes],
        ),
        out_shape=[jax.ShapeDtypeStruct(shape, jnp.float32) for shape in shapes],
        input_output_aliases={} if first else {at: 0, at + 1: 1},
        compiler_params=pltpu.CompilerParams(vmem_limit_bytes=VMEM_LIMIT),
        cost_estimate=SHORT,
        name="absorb",
    )(where, *operands)


def pick_kernel(choices, n_in, where, *refs):
    outs = refs[n_in:]
    for out, by_kind in zip(outs, choices):
        for source in sorted(set(by_kind), key=str):
            kinds = [kind for kind, chosen in enumerate(by_kind) if chosen == source]
            here = where[1] == kinds[0]
            for kind in kinds[1:]:
                here = here | (where[1] == kind)

            def send(out=out, source=source):
                if isinstance(source, int):
                    out[...] = refs[source][...]
                    return
                left = jnp.concatenate([refs[source[0]][...], refs[source[1]][...]], axis=0)
                for i in range(left.shape[0] // TILE):
                    for k in range(left.shape[1] // TILE):
                        out[k * TILE : (k + 1) * TILE, i * TILE : (i + 1) * TILE] = left[
                            i * TILE : (i + 1) * TILE, k * TILE : (k + 1) * TILE
                        ]

            pl.when(here)(send)


def pick(where, operands, specs, choices, shape):
    return pl.pallas_call(
        functools.partial(pick_kernel, choices, len(operands)),
        grid_spec=pltpu.PrefetchScalarGridSpec(
            num_scalar_prefetch=1,
            grid=(1,),
            in_specs=specs,
            out_specs=[pl.BlockSpec(shape.shape, lambda g, where: (0, 0))] * len(choices),
        ),
        out_shape=[shape] * len(choices),
        compiler_params=pltpu.CompilerParams(vmem_limit_bytes=VMEM_LIMIT),
        cost_estimate=SHORT,
        name="pick",
    )(where, *operands)


def help_kernel(rows, first, where, *refs):
    mine_out, theirs_out, left = refs[-3:]
    packed, slab = refs[:2]
    if first:
        mine_out[...] = jnp.zeros_like(mine_out)
        theirs_out[...] = jnp.zeros_like(theirs_out)
    else:
        mine_out[...] = refs[2][...]
        theirs_out[...] = refs[3][...]

    @pl.when(where[1] == 1)
    def _():
        depth, width = packed.shape
        for i in range(width // TILE):
            for k in range(depth // TILE):
                left[i * TILE : (i + 1) * TILE, k * TILE : (k + 1) * TILE] = packed[
                    k * TILE : (k + 1) * TILE, i * TILE : (i + 1) * TILE
                ]
        left[width:, :] = jnp.ones((ONES, depth), left.dtype)
        product = jnp.dot(left[...], slab[...], preferred_element_type=jnp.float32)
        mine_out[...] += product[:rows]
        theirs_out[...] += product[rows:]


def help_corner(where, packed, slab, rows, sums):
    depth, width = packed.shape
    shapes = [(rows, width), (rows + ONES, width)]
    first = sums is None
    operands = [packed, slab] + ([] if first else list(sums))

    def whole(shape):
        return pl.BlockSpec(shape, lambda g, where: (0, 0))

    return pl.pallas_call(
        functools.partial(help_kernel, rows, first),
        grid_spec=pltpu.PrefetchScalarGridSpec(
            num_scalar_prefetch=1,
            grid=(1,),
            in_specs=[whole((depth, width))] * 2 + ([] if first else [whole(s) for s in shapes]),
            out_specs=[whole(shape) for shape in shapes],
            scratch_shapes=[pltpu.VMEM((width + ONES, depth), packed.dtype)],
        ),
        out_shape=[jax.ShapeDtypeStruct(shape, jnp.float32) for shape in shapes],
        compiler_params=pltpu.CompilerParams(vmem_limit_bytes=VMEM_LIMIT),
        cost_estimate=SHORT,
        name="help",
    )(where, *operands)


def make_shards(n_row):
    chips = n_row // CORES
    cycle = chip_cycle(chips)
    place = {chip: k for k, chip in enumerate(cycle)}

    def walk(d):
        p = place[d // CORES]
        return p if d % CORES == 0 else chips - 1 - p

    def device(p, c):
        return cycle[p if c == 0 else chips - 1 - p] * CORES + c

    def pairs(route):
        return [(device(p, c), device(q, c)) for p, q in route.items() for c in range(CORES)]

    swap = [(d, d ^ 1) for d in range(n_row)]

    def shards(adj_rows, adj_panel, adj_tile):
        rows = adj_rows.shape[0]
        _, depth, width = adj_panel.shape
        ships = SHIPS and chips == 8 and 2 * rows == width and width % TILE == 0 and depth % TILE == 0
        turns = make_rounds(chips, ships)
        blocks = trace_blocks(chips, turns)
        rounds = len(turns)
        halves = range(CORES)

        groups = [[("own", 0)]] + [[(port, r) for port in turn] for r, turn in enumerate(turns, 1)]
        sources = [source for group in groups for source in group]
        if ships:
            sources = [("ship", 0), ("ship", 1)] + sources
        units, flags = {}, {}
        table = [[d % CORES, walk(d) % 4] for d in range(n_row)]
        for k, source in enumerate(sources):
            units[source] = [CORES * k + j for j in halves]
            for d in range(n_row):
                c = d % CORES
                p, other = blocks[source][walk(d)] or (walk(d), 0)
                owner = device(p, c) // CORES
                table[d] += [(c ^ other) * n_row + owner * CORES + (c ^ j) for j in halves]
        n_units = CORES * len(sources)
        table = [table[d] + table[d ^ 1][2:] for d in range(n_row)]
        for source in sources:
            flags[source] = None
            if source[0] == "main" and None in blocks[source]:
                flags[source] = len(table[0])
                for d in range(n_row):
                    table[d].append(int(blocks[source][walk(d)] is not None))
        me = lax.axis_index("row")
        where = jnp.asarray(np.array(table, np.int32))[me]
        core = lax.rem(me, CORES)

        def tie(values, others):
            return lax.optimization_barrier((values, others))[0]

        def exchange(value):
            return lax.ppermute(value, "row", swap)

        def depart(turn, j):
            sending = {}
            for port, chosen in turn.items():
                kinds = sorted(set(chosen))
                pieces = [(packed if source[0] == "ship" else slab)[source][j] for source in kinds]
                if len(kinds) == 1:
                    sending[port] = pieces[0]
                    continue
                specs = [pl.BlockSpec((depth, width), lambda g, where: (0, 0))] * len(pieces)
                choices = [[kinds.index(source) for source in chosen]]
                shape = jax.ShapeDtypeStruct((depth, width), adj_panel.dtype)
                sending[port] = pick(where, pieces, specs, choices, shape)[0]
            return sending

        def pack(source):
            shape = jax.ShapeDtypeStruct((depth, width), adj_panel.dtype)
            result = []
            for unit in units[source]:
                specs = [
                    pl.BlockSpec((rows, depth), lambda g, where, unit=unit: (0, where[2 + unit])),
                    pl.BlockSpec((rows, depth), lambda g, where, unit=unit: (0, unit % PER_LENT)),
                ]
                result += pick(where, [adj_rows, borrowed[unit // PER_LENT]], specs, [[(0, 1)] * 4], shape)
            return result

        here = lax.dynamic_index_in_dim(adj_panel, core, 0, keepdims=False)
        there = lax.dynamic_index_in_dim(adj_panel, 1 - core, 0, keepdims=False)
        slab = {("own", 0): [here, exchange(there)]}
        if ships:
            slab["own", 1] = [there, exchange(here)]
        sizes = [min(PER_LENT, n_units - k) for k in range(0, n_units, PER_LENT)]
        lent = lend(where, tie(adj_rows, slab["own", 0][LEND_AFTER]), sizes, 2 + n_units, depth)
        borrowed = [exchange(part) for part in lent[:EARLY]]
        packed = {("ship", k): pack(("ship", k)) for k in range(2)} if ships else {}
        sums, helped = None, None
        degree = []
        due = [(0, j) for j in halves]
        stretch = adj_rows.shape[1] // DEGREE_PARTS
        past = []
        for r in range(1, rounds + 2):
            for port in turns[r - 1] if r <= rounds else ():
                slab[port, r] = []
            for j in halves:
                at = r - 1
                if at > 0 and len(past) >= SLOTS:
                    arrived = tie([slab[port, at][j] for port in turns[at - 1]], past[-SLOTS])
                    for port, piece in zip(turns[at - 1], arrived):
                        slab[port, at][j] = piece
                if r <= rounds:
                    sending = depart(turns[r - 1], j)
                    for port, piece in sending.items():
                        slab[port, r].append(lax.ppermute(piece, "row", pairs(make_route(chips, port, r))))
                    if r == REST_AT and j == 0:
                        borrowed += [exchange(part) for part in tie(lent[EARLY:], list(sending.values()))]
                if at == 0:
                    continue
                gate = [slab[port, at][j] for port in turns[at - 1]]
                if r <= rounds:
                    gate = [gate, list(sending.values())]
                done = []
                past.append(done)
                due.append((at, j))
                if ships and at in HELP_AT:
                    beside = slab["own", 0] if at == HELP_AT[0] else slab["ch", 2]
                    helped = help_corner(where, slab["main", at][j], tie(beside[j], gate), rows, helped)
                    done.append(helped)
                    if (at, j) == (HELP_AT[1], 1):
                        back = lax.ppermute(jnp.concatenate(helped, axis=0), "row", pairs({1: 0, 5: 4}))
                if at >= ABSORB_FROM:
                    now = tie(adj_rows, gate)
                    for _ in range(MOST if r <= rounds else len(due)):
                        if due:
                            t, part = due.pop(0)
                            sums = absorb(
                                where,
                                now,
                                borrowed,
                                tie([slab[source][part] for source in groups[t]], gate),
                                [units[source][part] for source in groups[t]],
                                [flags[source] for source in groups[t]],
                                sums,
                            )
                            done.append(sums)
                if at >= DEGREE_AT and len(degree) < DEGREE_PARTS:
                    k = len(degree) * stretch
                    part = lax.slice_in_dim(tie(adj_rows, gate), k, k + stretch, axis=1)
                    degree.append(jnp.sum(part, axis=1, dtype=jnp.float32))
                    done.append(degree[-1])
        degree = sum(degree)

        mine, theirs = sums
        if ships:
            mine, theirs = mine + back[:rows], theirs + back[rows:]
        partner = exchange(theirs)
        square = mine + partner[:rows]
        col_degree = theirs[rows : rows + 1] + partner[rows : rows + 1]
        tile = adj_tile.astype(jnp.float32)
        lower = jnp.minimum(degree[:, None], col_degree)
        intersection = (square + tile) / (lower + 1.0 - tile)
        return (intersection, degree)

    return shards


def solution(mesh):
    in_specs = (
        P(("parts", "row"), None),
        P(None, ("parts", "row"), None),
        P(("parts", "row"), None),
    )
    out_specs = (P(("parts", "row"), None), P(("parts", "row")))
    return jax.shard_map(
        make_shards(mesh.shape["row"]), mesh=mesh, in_specs=in_specs, out_specs=out_specs, check_vma=False
    )
```

```python
import functools

import jax
import jax.numpy as jnp
import numpy as np
from jax import lax
from jax.experimental import pallas as pl
from jax.experimental.pallas import tpu as pltpu
from jax.sharding import PartitionSpec as P

CORES = 2
ONES = 16
SHIPS = True
SLOTS = 1
MOST = 2
ABSORB_FROM = 3
PER_LENT = 4
EARLY = 1
REST_AT = 2
DEGREE_PARTS = 4
DEGREE_AT = 1
HELP_AT = (3, 4)
LEND_AFTER = 0
TILE = 128
SHORT = pl.CostEstimate(flops=0, bytes_accessed=1024, transcendentals=0)
VMEM_LIMIT = 10 * 1024 * 1024
LEND_LIMIT = 44 * 1024 * 1024


def chip_cycle(chips):
    wide = 1
    while (2 * wide) ** 2 <= chips:
        wide *= 2
    high = chips // wide
    if wide == 1 or high % 2 or wide * high != chips:
        return list(range(chips))
    walk = [(0, 0)]
    for i in range(high):
        line = range(1, wide)
        walk += [(i, j) for j in (line if i % 2 == 0 else reversed(line))]
    walk += [(i, 0) for i in range(high - 1, 0, -1)]
    walk = walk[:1] + walk[:0:-1]
    return [i * wide + j for i, j in walk]


def make_rounds(chips, ships):
    count = 6 if ships else chips - 1
    main = [[("own", 0)] * 4] + [[("main", r)] * 4 for r in range(1, count)]
    turns = [{"main": sources} for sources in main]
    if ships:
        main[1][3] = ("own", 1)
        main[2][0] = ("ship", 0)
        main[3][0] = ("ship", 1)
        main[3][1] = ("ch", 2)
        main[4][1] = ("ch", 3)
        for r, source in ((1, ("own", 0)), (2, ("main", 1)), (3, ("main", 2)), (4, ("main", 4))):
            turns[r]["ch"] = [source] * 4
    return turns


def make_route(chips, port, r):
    if port == "main":
        return {p: (p + 1) % chips for p in range(chips)}
    return {1: 6, 5: 2} if r == 4 else {6: 1, 2: 5}


def trace_blocks(chips, turns):
    held = {("own", s): [(p, s) for p in range(chips)] for s in range(2)}
    corner = [p % 4 == 0 for p in range(chips)]
    for k, ahead in enumerate((1, 6)):
        held["ship", k] = [((p + ahead) % chips, 0) if corner[p] else None for p in range(chips)]
    for r, turn in enumerate(turns, 1):
        for port, sources in turn.items():
            held[port, r] = [None] * chips
            for p, q in make_route(chips, port, r).items():
                source = sources[p % 4]
                held[port, r][q] = None if source[0] == "ship" else held[source][p]
    return held


def lend_kernel(sizes, first, depth, where, rows_ref, *refs):
    sems = refs[-1]
    copies = []
    for part, size in enumerate(sizes):
        for k in range(size):
            unit = sum(sizes[:part]) + k
            start = pl.multiple_of(where[first + unit] * depth, 128)
            copies.append(
                pltpu.make_async_copy(
                    rows_ref.at[:, pl.ds(start, depth)],
                    refs[part].at[:, pl.ds(k * depth, depth)],
                    sems.at[unit],
                )
            )
    for copy in copies:
        copy.start()
    for copy in copies:
        copy.wait()


def lend(where, adj_rows, sizes, first, depth):
    rows = adj_rows.shape[0]
    return pl.pallas_call(
        functools.partial(lend_kernel, sizes, first, depth),
        in_specs=[pl.BlockSpec(memory_space=pltpu.SMEM), pl.BlockSpec(memory_space=pl.ANY)],
        out_specs=[pl.BlockSpec(memory_space=pltpu.VMEM)] * len(sizes),
        out_shape=[jax.ShapeDtypeStruct((rows, size * depth), adj_rows.dtype) for size in sizes],
        scratch_shapes=[pltpu.SemaphoreType.DMA((sum(sizes),))],
        compiler_params=pltpu.CompilerParams(vmem_limit_bytes=LEND_LIMIT),
        cost_estimate=SHORT,
        name="lend",
    )(where, adj_rows)


def absorb_kernel(count, flags, rows, first, where, *refs):
    own, other, slab = (refs[k * count : (k + 1) * count] for k in range(3))
    mine_out, theirs_out = refs[-2:]
    total = None
    for k in range(count):
        ones = jnp.ones((ONES, own[k].shape[1]), own[k].dtype)
        left = jnp.concatenate([own[k][...], other[k][...], ones], axis=0)
        product = jnp.dot(left, slab[k][...], preferred_element_type=jnp.float32)
        if flags[k] is not None:
            product = jnp.where(where[flags[k]] > 0, product, 0.0)
        total = product if total is None else total + product
    mine, theirs = total[:rows], total[rows:]
    if not first:
        mine_in, theirs_in = refs[3 * count : 3 * count + 2]
        mine, theirs = mine + mine_in[...], theirs + theirs_in[...]
    mine_out[...] = mine
    theirs_out[...] = theirs


def absorb(where, adj_rows, borrowed, slabs, units, flags, sums):
    count = len(slabs)
    rows = adj_rows.shape[0]
    depth, width = slabs[0].shape

    def own(k):
        return pl.BlockSpec((rows, depth), lambda g, where: (0, where[2 + units[k]]))

    def other(k):
        return pl.BlockSpec((rows, depth), lambda g, where: (0, units[k] % PER_LENT))

    def whole(shape):
        return pl.BlockSpec(shape, lambda g, where: (0, 0))

    shapes = [(rows, width), (rows + ONES, width)]
    first = sums is None
    operands = [adj_rows] * count + [borrowed[unit // PER_LENT] for unit in units] + list(slabs)
    in_specs = [own(k) for k in range(count)] + [other(k) for k in range(count)]
    in_specs += [whole((depth, width))] * count
    if not first:
        operands += list(sums)
        in_specs += [whole(shape) for shape in shapes]
    at = 1 + 3 * count
    return pl.pallas_call(
        functools.partial(absorb_kernel, count, flags, rows, first),
        grid_spec=pltpu.PrefetchScalarGridSpec(
            num_scalar_prefetch=1,
            grid=(1,),
            in_specs=in_specs,
            out_specs=[whole(shape) for shape in shapes],
        ),
        out_shape=[jax.ShapeDtypeStruct(shape, jnp.float32) for shape in shapes],
        input_output_aliases={} if first else {at: 0, at + 1: 1},
        compiler_params=pltpu.CompilerParams(vmem_limit_bytes=VMEM_LIMIT),
        cost_estimate=SHORT,
        name="absorb",
    )(where, *operands)


def pick_kernel(choices, n_in, where, *refs):
    outs = refs[n_in:]
    for out, by_kind in zip(outs, choices):
        for source in sorted(set(by_kind), key=str):
            kinds = [kind for kind, chosen in enumerate(by_kind) if chosen == source]
            here = where[1] == kinds[0]
            for kind in kinds[1:]:
                here = here | (where[1] == kind)

            def send(out=out, source=source):
                if isinstance(source, int):
                    out[...] = refs[source][...]
                    return
                left = jnp.concatenate([refs[source[0]][...], refs[source[1]][...]], axis=0)
                for i in range(left.shape[0] // TILE):
                    for k in range(left.shape[1] // TILE):
                        out[k * TILE : (k + 1) * TILE, i * TILE : (i + 1) * TILE] = left[
                            i * TILE : (i + 1) * TILE, k * TILE : (k + 1) * TILE
                        ]

            pl.when(here)(send)


def pick(where, operands, specs, choices, shape):
    return pl.pallas_call(
        functools.partial(pick_kernel, choices, len(operands)),
        grid_spec=pltpu.PrefetchScalarGridSpec(
            num_scalar_prefetch=1,
            grid=(1,),
            in_specs=specs,
            out_specs=[pl.BlockSpec(shape.shape, lambda g, where: (0, 0))] * len(choices),
        ),
        out_shape=[shape] * len(choices),
        compiler_params=pltpu.CompilerParams(vmem_limit_bytes=VMEM_LIMIT),
        cost_estimate=SHORT,
        name="pick",
    )(where, *operands)


def help_kernel(rows, first, where, *refs):
    mine_out, theirs_out, left = refs[-3:]
    packed, slab = refs[:2]
    if first:
        mine_out[...] = jnp.zeros_like(mine_out)
        theirs_out[...] = jnp.zeros_like(theirs_out)
    else:
        mine_out[...] = refs[2][...]
        theirs_out[...] = refs[3][...]

    @pl.when(where[1] == 1)
    def _():
        depth, width = packed.shape
        for i in range(width // TILE):
            for k in range(depth // TILE):
                left[i * TILE : (i + 1) * TILE, k * TILE : (k + 1) * TILE] = packed[
                    k * TILE : (k + 1) * TILE, i * TILE : (i + 1) * TILE
                ]
        left[width:, :] = jnp.ones((ONES, depth), left.dtype)
        product = jnp.dot(left[...], slab[...], preferred_element_type=jnp.float32)
        mine_out[...] += product[:rows]
        theirs_out[...] += product[rows:]


def help_corner(where, packed, slab, rows, sums):
    depth, width = packed.shape
    shapes = [(rows, width), (rows + ONES, width)]
    first = sums is None
    operands = [packed, slab] + ([] if first else list(sums))

    def whole(shape):
        return pl.BlockSpec(shape, lambda g, where: (0, 0))

    return pl.pallas_call(
        functools.partial(help_kernel, rows, first),
        grid_spec=pltpu.PrefetchScalarGridSpec(
            num_scalar_prefetch=1,
            grid=(1,),
            in_specs=[whole((depth, width))] * 2 + ([] if first else [whole(s) for s in shapes]),
            out_specs=[whole(shape) for shape in shapes],
            scratch_shapes=[pltpu.VMEM((width + ONES, depth), packed.dtype)],
        ),
        out_shape=[jax.ShapeDtypeStruct(shape, jnp.float32) for shape in shapes],
        compiler_params=pltpu.CompilerParams(vmem_limit_bytes=VMEM_LIMIT),
        cost_estimate=SHORT,
        name="help",
    )(where, *operands)


def make_shards(n_row):
    chips = n_row // CORES
    cycle = chip_cycle(chips)
    place = {chip: k for k, chip in enumerate(cycle)}

    def walk(d):
        p = place[d // CORES]
        return p if d % CORES == 0 else chips - 1 - p

    def device(p, c):
        return cycle[p if c == 0 else chips - 1 - p] * CORES + c

    def pairs(route):
        return [(device(p, c), device(q, c)) for p, q in route.items() for c in range(CORES)]

    swap = [(d, d ^ 1) for d in range(n_row)]

    def shards(adj_rows, adj_panel, adj_tile):
        rows = adj_rows.shape[0]
        _, depth, width = adj_panel.shape
        ships = SHIPS and chips == 8 and 2 * rows == width and width % TILE == 0 and depth % TILE == 0
        turns = make_rounds(chips, ships)
        blocks = trace_blocks(chips, turns)
        rounds = len(turns)
        halves = range(CORES)

        groups = [[("own", 0)]] + [[(port, r) for port in turn] for r, turn in enumerate(turns, 1)]
        sources = [source for group in groups for source in group]
        if ships:
            sources = [("ship", 0), ("ship", 1)] + sources
        units, flags = {}, {}
        table = [[d % CORES, walk(d) % 4] for d in range(n_row)]
        for k, source in enumerate(sources):
            units[source] = [CORES * k + j for j in halves]
            for d in range(n_row):
                c = d % CORES
                p, other = blocks[source][walk(d)] or (walk(d), 0)
                owner = device(p, c) // CORES
                table[d] += [(c ^ other) * n_row + owner * CORES + (c ^ j) for j in halves]
        n_units = CORES * len(sources)
        table = [table[d] + table[d ^ 1][2:] for d in range(n_row)]
        for source in sources:
            flags[source] = None
            if source[0] == "main" and None in blocks[source]:
                flags[source] = len(table[0])
                for d in range(n_row):
                    table[d].append(int(blocks[source][walk(d)] is not None))
        me = lax.axis_index("row")
        where = jnp.asarray(np.array(table, np.int32))[me]
        core = lax.rem(me, CORES)

        def tie(values, others):
            return lax.optimization_barrier((values, others))[0]

        def exchange(value):
            return lax.ppermute(value, "row", swap)

        def depart(turn, j):
            sending = {}
            for port, chosen in turn.items():
                kinds = sorted(set(chosen))
                pieces = [(packed if source[0] == "ship" else slab)[source][j] for source in kinds]
                if len(kinds) == 1:
                    sending[port] = pieces[0]
                    continue
                specs = [pl.BlockSpec((depth, width), lambda g, where: (0, 0))] * len(pieces)
                choices = [[kinds.index(source) for source in chosen]]
                shape = jax.ShapeDtypeStruct((depth, width), adj_panel.dtype)
                sending[port] = pick(where, pieces, specs, choices, shape)[0]
            return sending

        def pack(source):
            shape = jax.ShapeDtypeStruct((depth, width), adj_panel.dtype)
            result = []
            for unit in units[source]:
                specs = [
                    pl.BlockSpec((rows, depth), lambda g, where, unit=unit: (0, where[2 + unit])),
                    pl.BlockSpec((rows, depth), lambda g, where, unit=unit: (0, unit % PER_LENT)),
                ]
                result += pick(where, [adj_rows, borrowed[unit // PER_LENT]], specs, [[(0, 1)] * 4], shape)
            return result

        here = lax.dynamic_index_in_dim(adj_panel, core, 0, keepdims=False)
        there = lax.dynamic_index_in_dim(adj_panel, 1 - core, 0, keepdims=False)
        slab = {("own", 0): [here, exchange(there)]}
        if ships:
            slab["own", 1] = [there, exchange(here)]
        sizes = [min(PER_LENT, n_units - k) for k in range(0, n_units, PER_LENT)]
        lent = lend(where, tie(adj_rows, slab["own", 0][LEND_AFTER]), sizes, 2 + n_units, depth)
        borrowed = [exchange(part) for part in lent[:EARLY]]
        packed = {("ship", k): pack(("ship", k)) for k in range(2)} if ships else {}
        sums, helped = None, None
        degree = []
        due = [(0, j) for j in halves]
        stretch = adj_rows.shape[1] // DEGREE_PARTS
        past = []
        for r in range(1, rounds + 2):
            for port in turns[r - 1] if r <= rounds else ():
                slab[port, r] = []
            for j in halves:
                at = r - 1
                if at > 0 and len(past) >= SLOTS:
                    arrived = tie([slab[port, at][j] for port in turns[at - 1]], past[-SLOTS])
                    for port, piece in zip(turns[at - 1], arrived):
                        slab[port, at][j] = piece
                if r <= rounds:
                    sending = depart(turns[r - 1], j)
                    for port, piece in sending.items():
                        slab[port, r].append(lax.ppermute(piece, "row", pairs(make_route(chips, port, r))))
                    if r == REST_AT and j == 0:
                        borrowed += [exchange(part) for part in tie(lent[EARLY:], list(sending.values()))]
                if at == 0:
                    continue
                gate = [slab[port, at][j] for port in turns[at - 1]]
                if r <= rounds:
                    gate = [gate, list(sending.values())]
                done = []
                past.append(done)
                due.append((at, j))
                if ships and at in HELP_AT:
                    beside = slab["own", 0] if at == HELP_AT[0] else slab["ch", 2]
                    helped = help_corner(where, slab["main", at][j], tie(beside[j], gate), rows, helped)
                    done.append(helped)
                    if (at, j) == (HELP_AT[1], 1):
                        back = lax.ppermute(jnp.concatenate(helped, axis=0), "row", pairs({1: 0, 5: 4}))
                if at >= ABSORB_FROM:
                    now = tie(adj_rows, gate)
                    for _ in range(MOST if r <= rounds else len(due)):
                        if due:
                            t, part = due.pop(0)
                            sums = absorb(
                                where,
                                now,
                                borrowed,
                                tie([slab[source][part] for source in groups[t]], gate),
                                [units[source][part] for source in groups[t]],
                                [flags[source] for source in groups[t]],
                                sums,
                            )
                            done.append(sums)
                if at >= DEGREE_AT and len(degree) < DEGREE_PARTS:
                    k = len(degree) * stretch
                    part = lax.slice_in_dim(tie(adj_rows, gate), k, k + stretch, axis=1)
                    degree.append(jnp.sum(part, axis=1, dtype=jnp.float32))
                    done.append(degree[-1])
        degree = sum(degree)

        mine, theirs = sums
        if ships:
            mine, theirs = mine + back[:rows], theirs + back[rows:]
        partner = exchange(theirs)
        square = mine + partner[:rows]
        col_degree = theirs[rows : rows + 1] + partner[rows : rows + 1]
        tile = adj_tile.astype(jnp.float32)
        lower = jnp.minimum(degree[:, None], col_degree)
        intersection = (square + tile) / (lower + 1.0 - tile)
        return (intersection, degree)

    return shards


def solution(mesh):
    in_specs = (
        P(("parts", "row"), None),
        P(None, ("parts", "row"), None),
        P(("parts", "row"), None),
    )
    out_specs = (P(("parts", "row"), None), P(("parts", "row")))
    return jax.shard_map(
        make_shards(mesh.shape["row"]), mesh=mesh, in_specs=in_specs, out_specs=out_specs, check_vma=False
    )
```

```python
import functools

import jax
import jax.numpy as jnp
import numpy as np
from jax import lax
from jax.experimental import pallas as pl
from jax.experimental.pallas import tpu as pltpu
from jax.sharding import PartitionSpec as P

CORES = 2
ONES = 16
SHIPS = True
SLOTS = 1
MOST = 1
ABSORB_FROM = 2
PER_LENT = 4
EARLY = 1
REST_AT = 2
DEGREE_PARTS = 4
DEGREE_AT = 1
HELP_AT = (3, 4)
LEND_AFTER = 1
TILE = 128
SHORT = pl.CostEstimate(flops=0, bytes_accessed=1024, transcendentals=0)
VMEM_LIMIT = 10 * 1024 * 1024
LEND_LIMIT = 44 * 1024 * 1024


def chip_cycle(chips):
    wide = 1
    while (2 * wide) ** 2 <= chips:
        wide *= 2
    high = chips // wide
    if wide == 1 or high % 2 or wide * high != chips:
        return list(range(chips))
    walk = [(0, 0)]
    for i in range(high):
        line = range(1, wide)
        walk += [(i, j) for j in (line if i % 2 == 0 else reversed(line))]
    walk += [(i, 0) for i in range(high - 1, 0, -1)]
    walk = walk[:1] + walk[:0:-1]
    return [i * wide + j for i, j in walk]


def make_rounds(chips, ships):
    count = 6 if ships else chips - 1
    main = [[("own", 0)] * 4] + [[("main", r)] * 4 for r in range(1, count)]
    turns = [{"main": sources} for sources in main]
    if ships:
        main[1][3] = ("own", 1)
        main[2][0] = ("ship", 0)
        main[3][0] = ("ship", 1)
        main[3][1] = ("ch", 1)
        main[4][1] = ("ch", 2)
        for r, source in ((0, ("own", 0)), (1, ("main", 1)), (2, ("main", 2)), (4, ("main", 4))):
            turns[r]["ch"] = [source] * 4
    return turns


def make_route(chips, port, r):
    if port == "main":
        return {p: (p + 1) % chips for p in range(chips)}
    return {1: 6, 5: 2} if r == 3 else {6: 1, 2: 5}


def trace_blocks(chips, turns):
    held = {("own", s): [(p, s) for p in range(chips)] for s in range(2)}
    corner = [p % 4 == 0 for p in range(chips)]
    for k, ahead in enumerate((1, 6)):
        held["ship", k] = [((p + ahead) % chips, 0) if corner[p] else None for p in range(chips)]
    for r, turn in enumerate(turns, 1):
        for port, sources in turn.items():
            held[port, r] = [None] * chips
            for p, q in make_route(chips, port, r).items():
                source = sources[p % 4]
                held[port, r][q] = None if source[0] == "ship" else held[source][p]
    return held


def lend_kernel(sizes, first, depth, where, rows_ref, *refs):
    sems = refs[-1]
    copies = []
    for part, size in enumerate(sizes):
        for k in range(size):
            unit = sum(sizes[:part]) + k
            start = pl.multiple_of(where[first + unit] * depth, 128)
            copies.append(
                pltpu.make_async_copy(
                    rows_ref.at[:, pl.ds(start, depth)],
                    refs[part].at[:, pl.ds(k * depth, depth)],
                    sems.at[unit],
                )
            )
    for copy in copies:
        copy.start()
    for copy in copies:
        copy.wait()


def lend(where, adj_rows, sizes, first, depth):
    rows = adj_rows.shape[0]
    return pl.pallas_call(
        functools.partial(lend_kernel, sizes, first, depth),
        in_specs=[pl.BlockSpec(memory_space=pltpu.SMEM), pl.BlockSpec(memory_space=pl.ANY)],
        out_specs=[pl.BlockSpec(memory_space=pltpu.VMEM)] * len(sizes),
        out_shape=[jax.ShapeDtypeStruct((rows, size * depth), adj_rows.dtype) for size in sizes],
        scratch_shapes=[pltpu.SemaphoreType.DMA((sum(sizes),))],
        compiler_params=pltpu.CompilerParams(vmem_limit_bytes=LEND_LIMIT),
        cost_estimate=SHORT,
        name="lend",
    )(where, adj_rows)


def absorb_kernel(count, flags, rows, first, where, *refs):
    own, other, slab = (refs[k * count : (k + 1) * count] for k in range(3))
    mine_out, theirs_out = refs[-2:]
    total = None
    for k in range(count):
        ones = jnp.ones((ONES, own[k].shape[1]), own[k].dtype)
        left = jnp.concatenate([own[k][...], other[k][...], ones], axis=0)
        product = jnp.dot(left, slab[k][...], preferred_element_type=jnp.float32)
        if flags[k] is not None:
            product = jnp.where(where[flags[k]] > 0, product, 0.0)
        total = product if total is None else total + product
    mine, theirs = total[:rows], total[rows:]
    if not first:
        mine_in, theirs_in = refs[3 * count : 3 * count + 2]
        mine, theirs = mine + mine_in[...], theirs + theirs_in[...]
    mine_out[...] = mine
    theirs_out[...] = theirs


def absorb(where, adj_rows, borrowed, slabs, units, flags, sums):
    count = len(slabs)
    rows = adj_rows.shape[0]
    depth, width = slabs[0].shape

    def own(k):
        return pl.BlockSpec((rows, depth), lambda g, where: (0, where[2 + units[k]]))

    def other(k):
        return pl.BlockSpec((rows, depth), lambda g, where: (0, units[k] % PER_LENT))

    def whole(shape):
        return pl.BlockSpec(shape, lambda g, where: (0, 0))

    shapes = [(rows, width), (rows + ONES, width)]
    first = sums is None
    operands = [adj_rows] * count + [borrowed[unit // PER_LENT] for unit in units] + list(slabs)
    in_specs = [own(k) for k in range(count)] + [other(k) for k in range(count)]
    in_specs += [whole((depth, width))] * count
    if not first:
        operands += list(sums)
        in_specs += [whole(shape) for shape in shapes]
    at = 1 + 3 * count
    return pl.pallas_call(
        functools.partial(absorb_kernel, count, flags, rows, first),
        grid_spec=pltpu.PrefetchScalarGridSpec(
            num_scalar_prefetch=1,
            grid=(1,),
            in_specs=in_specs,
            out_specs=[whole(shape) for shape in shapes],
        ),
        out_shape=[jax.ShapeDtypeStruct(shape, jnp.float32) for shape in shapes],
        input_output_aliases={} if first else {at: 0, at + 1: 1},
        compiler_params=pltpu.CompilerParams(vmem_limit_bytes=VMEM_LIMIT),
        cost_estimate=SHORT,
        name="absorb",
    )(where, *operands)


def pick_kernel(choices, n_in, where, *refs):
    outs = refs[n_in:]
    for out, by_kind in zip(outs, choices):
        for source in sorted(set(by_kind), key=str):
            kinds = [kind for kind, chosen in enumerate(by_kind) if chosen == source]
            here = where[1] == kinds[0]
            for kind in kinds[1:]:
                here = here | (where[1] == kind)

            def send(out=out, source=source):
                if isinstance(source, int):
                    out[...] = refs[source][...]
                    return
                left = jnp.concatenate([refs[source[0]][...], refs[source[1]][...]], axis=0)
                for i in range(left.shape[0] // TILE):
                    for k in range(left.shape[1] // TILE):
                        out[k * TILE : (k + 1) * TILE, i * TILE : (i + 1) * TILE] = left[
                            i * TILE : (i + 1) * TILE, k * TILE : (k + 1) * TILE
                        ]

            pl.when(here)(send)


def pick(where, operands, specs, choices, shape):
    return pl.pallas_call(
        functools.partial(pick_kernel, choices, len(operands)),
        grid_spec=pltpu.PrefetchScalarGridSpec(
            num_scalar_prefetch=1,
            grid=(1,),
            in_specs=specs,
            out_specs=[pl.BlockSpec(shape.shape, lambda g, where: (0, 0))] * len(choices),
        ),
        out_shape=[shape] * len(choices),
        compiler_params=pltpu.CompilerParams(vmem_limit_bytes=VMEM_LIMIT),
        cost_estimate=SHORT,
        name="pick",
    )(where, *operands)


def help_kernel(rows, first, where, *refs):
    mine_out, theirs_out, left = refs[-3:]
    packed, slab = refs[:2]
    if first:
        mine_out[...] = jnp.zeros_like(mine_out)
        theirs_out[...] = jnp.zeros_like(theirs_out)
    else:
        mine_out[...] = refs[2][...]
        theirs_out[...] = refs[3][...]

    @pl.when(where[1] == 1)
    def _():
        depth, width = packed.shape
        for i in range(width // TILE):
            for k in range(depth // TILE):
                left[i * TILE : (i + 1) * TILE, k * TILE : (k + 1) * TILE] = packed[
                    k * TILE : (k + 1) * TILE, i * TILE : (i + 1) * TILE
                ]
        left[width:, :] = jnp.ones((ONES, depth), left.dtype)
        product = jnp.dot(left[...], slab[...], preferred_element_type=jnp.float32)
        mine_out[...] += product[:rows]
        theirs_out[...] += product[rows:]


def help_corner(where, packed, slab, rows, sums):
    depth, width = packed.shape
    shapes = [(rows, width), (rows + ONES, width)]
    first = sums is None
    operands = [packed, slab] + ([] if first else list(sums))

    def whole(shape):
        return pl.BlockSpec(shape, lambda g, where: (0, 0))

    return pl.pallas_call(
        functools.partial(help_kernel, rows, first),
        grid_spec=pltpu.PrefetchScalarGridSpec(
            num_scalar_prefetch=1,
            grid=(1,),
            in_specs=[whole((depth, width))] * 2 + ([] if first else [whole(s) for s in shapes]),
            out_specs=[whole(shape) for shape in shapes],
            scratch_shapes=[pltpu.VMEM((width + ONES, depth), packed.dtype)],
        ),
        out_shape=[jax.ShapeDtypeStruct(shape, jnp.float32) for shape in shapes],
        compiler_params=pltpu.CompilerParams(vmem_limit_bytes=VMEM_LIMIT),
        cost_estimate=SHORT,
        name="help",
    )(where, *operands)


def make_shards(n_row):
    chips = n_row // CORES
    cycle = chip_cycle(chips)
    place = {chip: k for k, chip in enumerate(cycle)}

    def walk(d):
        p = place[d // CORES]
        return p if d % CORES == 0 else chips - 1 - p

    def device(p, c):
        return cycle[p if c == 0 else chips - 1 - p] * CORES + c

    def pairs(route):
        return [(device(p, c), device(q, c)) for p, q in route.items() for c in range(CORES)]

    swap = [(d, d ^ 1) for d in range(n_row)]

    def shards(adj_rows, adj_panel, adj_tile):
        rows = adj_rows.shape[0]
        _, depth, width = adj_panel.shape
        ships = SHIPS and chips == 8 and 2 * rows == width and width % TILE == 0 and depth % TILE == 0
        turns = make_rounds(chips, ships)
        blocks = trace_blocks(chips, turns)
        rounds = len(turns)
        halves = range(CORES)

        groups = [[("own", 0)]] + [[(port, r) for port in turn] for r, turn in enumerate(turns, 1)]
        sources = [source for group in groups for source in group]
        if ships:
            sources = [("ship", 0), ("ship", 1)] + sources
        units, flags = {}, {}
        table = [[d % CORES, walk(d) % 4] for d in range(n_row)]
        for k, source in enumerate(sources):
            units[source] = [CORES * k + j for j in halves]
            for d in range(n_row):
                c = d % CORES
                p, other = blocks[source][walk(d)] or (walk(d), 0)
                owner = device(p, c) // CORES
                table[d] += [(c ^ other) * n_row + owner * CORES + (c ^ j) for j in halves]
        n_units = CORES * len(sources)
        table = [table[d] + table[d ^ 1][2:] for d in range(n_row)]
        for source in sources:
            flags[source] = None
            if source[0] == "main" and None in blocks[source]:
                flags[source] = len(table[0])
                for d in range(n_row):
                    table[d].append(int(blocks[source][walk(d)] is not None))
        me = lax.axis_index("row")
        where = jnp.asarray(np.array(table, np.int32))[me]
        core = lax.rem(me, CORES)

        def tie(values, others):
            return lax.optimization_barrier((values, others))[0]

        def exchange(value):
            return lax.ppermute(value, "row", swap)

        def depart(turn, j):
            sending = {}
            for port, chosen in turn.items():
                kinds = sorted(set(chosen))
                pieces = [(packed if source[0] == "ship" else slab)[source][j] for source in kinds]
                if len(kinds) == 1:
                    sending[port] = pieces[0]
                    continue
                specs = [pl.BlockSpec((depth, width), lambda g, where: (0, 0))] * len(pieces)
                choices = [[kinds.index(source) for source in chosen]]
                shape = jax.ShapeDtypeStruct((depth, width), adj_panel.dtype)
                sending[port] = pick(where, pieces, specs, choices, shape)[0]
            return sending

        def pack(source):
            shape = jax.ShapeDtypeStruct((depth, width), adj_panel.dtype)
            result = []
            for unit in units[source]:
                specs = [
                    pl.BlockSpec((rows, depth), lambda g, where, unit=unit: (0, where[2 + unit])),
                    pl.BlockSpec((rows, depth), lambda g, where, unit=unit: (0, unit % PER_LENT)),
                ]
                result += pick(where, [adj_rows, borrowed[unit // PER_LENT]], specs, [[(0, 1)] * 4], shape)
            return result

        here = lax.dynamic_index_in_dim(adj_panel, core, 0, keepdims=False)
        there = lax.dynamic_index_in_dim(adj_panel, 1 - core, 0, keepdims=False)
        slab = {("own", 0): [here, exchange(there)]}
        if ships:
            slab["own", 1] = [there, exchange(here)]
        sizes = [min(PER_LENT, n_units - k) for k in range(0, n_units, PER_LENT)]
        lent = lend(where, tie(adj_rows, slab["own", 0][LEND_AFTER]), sizes, 2 + n_units, depth)
        borrowed = [exchange(part) for part in lent[:EARLY]]
        packed = {("ship", k): pack(("ship", k)) for k in range(2)} if ships else {}
        sums, helped = None, None
        degree = []
        due = [(0, j) for j in halves]
        stretch = adj_rows.shape[1] // DEGREE_PARTS
        past = []
        for r in range(1, rounds + 2):
            for port in turns[r - 1] if r <= rounds else ():
                slab[port, r] = []
            for j in halves:
                at = r - 1
                if at > 0 and len(past) >= SLOTS:
                    arrived = tie([slab[port, at][j] for port in turns[at - 1]], past[-SLOTS])
                    for port, piece in zip(turns[at - 1], arrived):
                        slab[port, at][j] = piece
                if r <= rounds:
                    sending = depart(turns[r - 1], j)
                    for port, piece in sending.items():
                        slab[port, r].append(lax.ppermute(piece, "row", pairs(make_route(chips, port, r))))
                    if r == REST_AT and j == 0:
                        borrowed += [exchange(part) for part in tie(lent[EARLY:], list(sending.values()))]
                if at == 0:
                    continue
                gate = [slab[port, at][j] for port in turns[at - 1]]
                if r <= rounds:
                    gate = [gate, list(sending.values())]
                done = []
                past.append(done)
                due.append((at, j))
                if ships and at in HELP_AT:
                    beside = slab["own", 0] if at == HELP_AT[0] else slab["ch", 1]
                    helped = help_corner(where, slab["main", at][j], tie(beside[j], gate), rows, helped)
                    done.append(helped)
                    if (at, j) == (HELP_AT[1], 1):
                        back = lax.ppermute(jnp.concatenate(helped, axis=0), "row", pairs({1: 0, 5: 4}))
                if at >= ABSORB_FROM:
                    now = tie(adj_rows, gate)
                    for _ in range(MOST if r <= rounds else len(due)):
                        if due:
                            t, part = due.pop(0)
                            sums = absorb(
                                where,
                                now,
                                borrowed,
                                tie([slab[source][part] for source in groups[t]], gate),
                                [units[source][part] for source in groups[t]],
                                [flags[source] for source in groups[t]],
                                sums,
                            )
                            done.append(sums)
                if at >= DEGREE_AT and len(degree) < DEGREE_PARTS:
                    k = len(degree) * stretch
                    part = lax.slice_in_dim(tie(adj_rows, gate), k, k + stretch, axis=1)
                    degree.append(jnp.sum(part, axis=1, dtype=jnp.float32))
                    done.append(degree[-1])
        degree = sum(degree)

        mine, theirs = sums
        if ships:
            mine, theirs = mine + back[:rows], theirs + back[rows:]
        partner = exchange(theirs)
        square = mine + partner[:rows]
        col_degree = theirs[rows : rows + 1] + partner[rows : rows + 1]
        tile = adj_tile.astype(jnp.float32)
        lower = jnp.minimum(degree[:, None], col_degree)
        intersection = (square + tile) / (lower + 1.0 - tile)
        return (intersection, degree)

    return shards


def solution(mesh):
    in_specs = (
        P(("parts", "row"), None),
        P(None, ("parts", "row"), None),
        P(("parts", "row"), None),
    )
    out_specs = (P(("parts", "row"), None), P(("parts", "row")))
    return jax.shard_map(
        make_shards(mesh.shape["row"]), mesh=mesh, in_specs=in_specs, out_specs=out_specs, check_vma=False
    )
```

```python
import functools

import jax
import jax.numpy as jnp
import numpy as np
from jax import lax
from jax.experimental import pallas as pl
from jax.experimental.pallas import tpu as pltpu
from jax.sharding import PartitionSpec as P

CORES = 2
ONES = 16
SHIPS = False
SLOTS = 1
MOST = 2
ABSORB_FROM = 3
PER_LENT = 4
EARLY = 1
REST_AT = 2
DEGREE_PARTS = 4
DEGREE_AT = 2
HELP_AT = (3, 4)
LEND_AFTER = 1
TILE = 128
SHORT = pl.CostEstimate(flops=0, bytes_accessed=1024, transcendentals=0)
VMEM_LIMIT = 10 * 1024 * 1024
LEND_LIMIT = 44 * 1024 * 1024


def chip_cycle(chips):
    wide = 1
    while (2 * wide) ** 2 <= chips:
        wide *= 2
    high = chips // wide
    if wide == 1 or high % 2 or wide * high != chips:
        return list(range(chips))
    walk = [(0, 0)]
    for i in range(high):
        line = range(1, wide)
        walk += [(i, j) for j in (line if i % 2 == 0 else reversed(line))]
    walk += [(i, 0) for i in range(high - 1, 0, -1)]
    walk = walk[:1] + walk[:0:-1]
    return [i * wide + j for i, j in walk]


def make_rounds(chips, ships):
    count = 6 if ships else chips - 1
    main = [[("own", 0)] * 4] + [[("main", r)] * 4 for r in range(1, count)]
    turns = [{"main": sources} for sources in main]
    if ships:
        main[1][3] = ("own", 1)
        main[2][0] = ("ship", 0)
        main[3][0] = ("ship", 1)
        main[3][1] = ("ch", 1)
        main[4][1] = ("ch", 2)
        for r, source in ((0, ("own", 0)), (1, ("main", 1)), (2, ("main", 2)), (4, ("main", 4))):
            turns[r]["ch"] = [source] * 4
    return turns


def make_route(chips, port, r):
    if port == "main":
        return {p: (p + 1) % chips for p in range(chips)}
    return {1: 6, 5: 2} if r == 3 else {6: 1, 2: 5}


def trace_blocks(chips, turns):
    held = {("own", s): [(p, s) for p in range(chips)] for s in range(2)}
    corner = [p % 4 == 0 for p in range(chips)]
    for k, ahead in enumerate((1, 6)):
        held["ship", k] = [((p + ahead) % chips, 0) if corner[p] else None for p in range(chips)]
    for r, turn in enumerate(turns, 1):
        for port, sources in turn.items():
            held[port, r] = [None] * chips
            for p, q in make_route(chips, port, r).items():
                source = sources[p % 4]
                held[port, r][q] = None if source[0] == "ship" else held[source][p]
    return held


def lend_kernel(sizes, first, depth, where, rows_ref, *refs):
    sems = refs[-1]
    copies = []
    for part, size in enumerate(sizes):
        for k in range(size):
            unit = sum(sizes[:part]) + k
            start = pl.multiple_of(where[first + unit] * depth, 128)
            copies.append(
                pltpu.make_async_copy(
                    rows_ref.at[:, pl.ds(start, depth)],
                    refs[part].at[:, pl.ds(k * depth, depth)],
                    sems.at[unit],
                )
            )
    for copy in copies:
        copy.start()
    for copy in copies:
        copy.wait()


def lend(where, adj_rows, sizes, first, depth):
    rows = adj_rows.shape[0]
    return pl.pallas_call(
        functools.partial(lend_kernel, sizes, first, depth),
        in_specs=[pl.BlockSpec(memory_space=pltpu.SMEM), pl.BlockSpec(memory_space=pl.ANY)],
        out_specs=[pl.BlockSpec(memory_space=pltpu.VMEM)] * len(sizes),
        out_shape=[jax.ShapeDtypeStruct((rows, size * depth), adj_rows.dtype) for size in sizes],
        scratch_shapes=[pltpu.SemaphoreType.DMA((sum(sizes),))],
        compiler_params=pltpu.CompilerParams(vmem_limit_bytes=LEND_LIMIT),
        cost_estimate=SHORT,
        name="lend",
    )(where, adj_rows)


def absorb_kernel(count, flags, rows, first, where, *refs):
    own, other, slab = (refs[k * count : (k + 1) * count] for k in range(3))
    mine_out, theirs_out = refs[-2:]
    total = None
    for k in range(count):
        ones = jnp.ones((ONES, own[k].shape[1]), own[k].dtype)
        left = jnp.concatenate([own[k][...], other[k][...], ones], axis=0)
        product = jnp.dot(left, slab[k][...], preferred_element_type=jnp.float32)
        if flags[k] is not None:
            product = jnp.where(where[flags[k]] > 0, product, 0.0)
        total = product if total is None else total + product
    mine, theirs = total[:rows], total[rows:]
    if not first:
        mine_in, theirs_in = refs[3 * count : 3 * count + 2]
        mine, theirs = mine + mine_in[...], theirs + theirs_in[...]
    mine_out[...] = mine
    theirs_out[...] = theirs


def absorb(where, adj_rows, borrowed, slabs, units, flags, sums):
    count = len(slabs)
    rows = adj_rows.shape[0]
    depth, width = slabs[0].shape

    def own(k):
        return pl.BlockSpec((rows, depth), lambda g, where: (0, where[2 + units[k]]))

    def other(k):
        return pl.BlockSpec((rows, depth), lambda g, where: (0, units[k] % PER_LENT))

    def whole(shape):
        return pl.BlockSpec(shape, lambda g, where: (0, 0))

    shapes = [(rows, width), (rows + ONES, width)]
    first = sums is None
    operands = [adj_rows] * count + [borrowed[unit // PER_LENT] for unit in units] + list(slabs)
    in_specs = [own(k) for k in range(count)] + [other(k) for k in range(count)]
    in_specs += [whole((depth, width))] * count
    if not first:
        operands += list(sums)
        in_specs += [whole(shape) for shape in shapes]
    at = 1 + 3 * count
    return pl.pallas_call(
        functools.partial(absorb_kernel, count, flags, rows, first),
        grid_spec=pltpu.PrefetchScalarGridSpec(
            num_scalar_prefetch=1,
            grid=(1,),
            in_specs=in_specs,
            out_specs=[whole(shape) for shape in shapes],
        ),
        out_shape=[jax.ShapeDtypeStruct(shape, jnp.float32) for shape in shapes],
        input_output_aliases={} if first else {at: 0, at + 1: 1},
        compiler_params=pltpu.CompilerParams(vmem_limit_bytes=VMEM_LIMIT),
        cost_estimate=SHORT,
        name="absorb",
    )(where, *operands)


def pick_kernel(choices, n_in, where, *refs):
    outs = refs[n_in:]
    for out, by_kind in zip(outs, choices):
        for source in sorted(set(by_kind), key=str):
            kinds = [kind for kind, chosen in enumerate(by_kind) if chosen == source]
            here = where[1] == kinds[0]
            for kind in kinds[1:]:
                here = here | (where[1] == kind)

            def send(out=out, source=source):
                if isinstance(source, int):
                    out[...] = refs[source][...]
                    return
                left = jnp.concatenate([refs[source[0]][...], refs[source[1]][...]], axis=0)
                for i in range(left.shape[0] // TILE):
                    for k in range(left.shape[1] // TILE):
                        out[k * TILE : (k + 1) * TILE, i * TILE : (i + 1) * TILE] = left[
                            i * TILE : (i + 1) * TILE, k * TILE : (k + 1) * TILE
                        ]

            pl.when(here)(send)


def pick(where, operands, specs, choices, shape):
    return pl.pallas_call(
        functools.partial(pick_kernel, choices, len(operands)),
        grid_spec=pltpu.PrefetchScalarGridSpec(
            num_scalar_prefetch=1,
            grid=(1,),
            in_specs=specs,
            out_specs=[pl.BlockSpec(shape.shape, lambda g, where: (0, 0))] * len(choices),
        ),
        out_shape=[shape] * len(choices),
        compiler_params=pltpu.CompilerParams(vmem_limit_bytes=VMEM_LIMIT),
        cost_estimate=SHORT,
        name="pick",
    )(where, *operands)


def help_kernel(rows, first, where, *refs):
    mine_out, theirs_out, left = refs[-3:]
    packed, slab = refs[:2]
    if first:
        mine_out[...] = jnp.zeros_like(mine_out)
        theirs_out[...] = jnp.zeros_like(theirs_out)
    else:
        mine_out[...] = refs[2][...]
        theirs_out[...] = refs[3][...]

    @pl.when(where[1] == 1)
    def _():
        depth, width = packed.shape
        for i in range(width // TILE):
            for k in range(depth // TILE):
                left[i * TILE : (i + 1) * TILE, k * TILE : (k + 1) * TILE] = packed[
                    k * TILE : (k + 1) * TILE, i * TILE : (i + 1) * TILE
                ]
        left[width:, :] = jnp.ones((ONES, depth), left.dtype)
        product = jnp.dot(left[...], slab[...], preferred_element_type=jnp.float32)
        mine_out[...] += product[:rows]
        theirs_out[...] += product[rows:]


def help_corner(where, packed, slab, rows, sums):
    depth, width = packed.shape
    shapes = [(rows, width), (rows + ONES, width)]
    first = sums is None
    operands = [packed, slab] + ([] if first else list(sums))

    def whole(shape):
        return pl.BlockSpec(shape, lambda g, where: (0, 0))

    return pl.pallas_call(
        functools.partial(help_kernel, rows, first),
        grid_spec=pltpu.PrefetchScalarGridSpec(
            num_scalar_prefetch=1,
            grid=(1,),
            in_specs=[whole((depth, width))] * 2 + ([] if first else [whole(s) for s in shapes]),
            out_specs=[whole(shape) for shape in shapes],
            scratch_shapes=[pltpu.VMEM((width + ONES, depth), packed.dtype)],
        ),
        out_shape=[jax.ShapeDtypeStruct(shape, jnp.float32) for shape in shapes],
        compiler_params=pltpu.CompilerParams(vmem_limit_bytes=VMEM_LIMIT),
        cost_estimate=SHORT,
        name="help",
    )(where, *operands)


def make_shards(n_row):
    chips = n_row // CORES
    cycle = chip_cycle(chips)
    place = {chip: k for k, chip in enumerate(cycle)}

    def walk(d):
        p = place[d // CORES]
        return p if d % CORES == 0 else chips - 1 - p

    def device(p, c):
        return cycle[p if c == 0 else chips - 1 - p] * CORES + c

    def pairs(route):
        return [(device(p, c), device(q, c)) for p, q in route.items() for c in range(CORES)]

    swap = [(d, d ^ 1) for d in range(n_row)]

    def shards(adj_rows, adj_panel, adj_tile):
        rows = adj_rows.shape[0]
        _, depth, width = adj_panel.shape
        ships = SHIPS and chips == 8 and 2 * rows == width and width % TILE == 0 and depth % TILE == 0
        turns = make_rounds(chips, ships)
        blocks = trace_blocks(chips, turns)
        rounds = len(turns)
        halves = range(CORES)

        groups = [[("own", 0)]] + [[(port, r) for port in turn] for r, turn in enumerate(turns, 1)]
        sources = [source for group in groups for source in group]
        if ships:
            sources = [("ship", 0), ("ship", 1)] + sources
        units, flags = {}, {}
        table = [[d % CORES, walk(d) % 4] for d in range(n_row)]
        for k, source in enumerate(sources):
            units[source] = [CORES * k + j for j in halves]
            for d in range(n_row):
                c = d % CORES
                p, other = blocks[source][walk(d)] or (walk(d), 0)
                owner = device(p, c) // CORES
                table[d] += [(c ^ other) * n_row + owner * CORES + (c ^ j) for j in halves]
        n_units = CORES * len(sources)
        table = [table[d] + table[d ^ 1][2:] for d in range(n_row)]
        for source in sources:
            flags[source] = None
            if source[0] == "main" and None in blocks[source]:
                flags[source] = len(table[0])
                for d in range(n_row):
                    table[d].append(int(blocks[source][walk(d)] is not None))
        me = lax.axis_index("row")
        where = jnp.asarray(np.array(table, np.int32))[me]
        core = lax.rem(me, CORES)

        def tie(values, others):
            return lax.optimization_barrier((values, others))[0]

        def exchange(value):
            return lax.ppermute(value, "row", swap)

        def depart(turn, j):
            sending = {}
            for port, chosen in turn.items():
                kinds = sorted(set(chosen))
                pieces = [(packed if source[0] == "ship" else slab)[source][j] for source in kinds]
                if len(kinds) == 1:
                    sending[port] = pieces[0]
                    continue
                specs = [pl.BlockSpec((depth, width), lambda g, where: (0, 0))] * len(pieces)
                choices = [[kinds.index(source) for source in chosen]]
                shape = jax.ShapeDtypeStruct((depth, width), adj_panel.dtype)
                sending[port] = pick(where, pieces, specs, choices, shape)[0]
            return sending

        def pack(source):
            shape = jax.ShapeDtypeStruct((depth, width), adj_panel.dtype)
            result = []
            for unit in units[source]:
                specs = [
                    pl.BlockSpec((rows, depth), lambda g, where, unit=unit: (0, where[2 + unit])),
                    pl.BlockSpec((rows, depth), lambda g, where, unit=unit: (0, unit % PER_LENT)),
                ]
                result += pick(where, [adj_rows, borrowed[unit // PER_LENT]], specs, [[(0, 1)] * 4], shape)
            return result

        here = lax.dynamic_index_in_dim(adj_panel, core, 0, keepdims=False)
        there = lax.dynamic_index_in_dim(adj_panel, 1 - core, 0, keepdims=False)
        slab = {("own", 0): [here, exchange(there)]}
        if ships:
            slab["own", 1] = [there, exchange(here)]
        sizes = [min(PER_LENT, n_units - k) for k in range(0, n_units, PER_LENT)]
        lent = lend(where, tie(adj_rows, slab["own", 0][LEND_AFTER]), sizes, 2 + n_units, depth)
        borrowed = [exchange(part) for part in lent[:EARLY]]
        packed = {("ship", k): pack(("ship", k)) for k in range(2)} if ships else {}
        sums, helped = None, None
        degree = []
        due = [(0, j) for j in halves]
        stretch = adj_rows.shape[1] // DEGREE_PARTS
        past = []
        for r in range(1, rounds + 2):
            for port in turns[r - 1] if r <= rounds else ():
                slab[port, r] = []
            for j in halves:
                at = r - 1
                if at > 0 and len(past) >= SLOTS:
                    arrived = tie([slab[port, at][j] for port in turns[at - 1]], past[-SLOTS])
                    for port, piece in zip(turns[at - 1], arrived):
                        slab[port, at][j] = piece
                if r <= rounds:
                    sending = depart(turns[r - 1], j)
                    for port, piece in sending.items():
                        slab[port, r].append(lax.ppermute(piece, "row", pairs(make_route(chips, port, r))))
                    if r == REST_AT and j == 0:
                        borrowed += [exchange(part) for part in tie(lent[EARLY:], list(sending.values()))]
                if at == 0:
                    continue
                gate = [slab[port, at][j] for port in turns[at - 1]]
                if r <= rounds:
                    gate = [gate, list(sending.values())]
                done = []
                past.append(done)
                due.append((at, j))
                if ships and at in HELP_AT:
                    beside = slab["own", 0] if at == HELP_AT[0] else slab["ch", 1]
                    helped = help_corner(where, slab["main", at][j], tie(beside[j], gate), rows, helped)
                    done.append(helped)
                    if (at, j) == (HELP_AT[1], 1):
                        back = lax.ppermute(jnp.concatenate(helped, axis=0), "row", pairs({1: 0, 5: 4}))
                if at >= ABSORB_FROM:
                    now = tie(adj_rows, gate)
                    for _ in range(MOST if r <= rounds else len(due)):
                        if due:
                            t, part = due.pop(0)
                            sums = absorb(
                                where,
                                now,
                                borrowed,
                                tie([slab[source][part] for source in groups[t]], gate),
                                [units[source][part] for source in groups[t]],
                                [flags[source] for source in groups[t]],
                                sums,
                            )
                            done.append(sums)
                if at >= DEGREE_AT and len(degree) < DEGREE_PARTS:
                    k = len(degree) * stretch
                    part = lax.slice_in_dim(tie(adj_rows, gate), k, k + stretch, axis=1)
                    degree.append(jnp.sum(part, axis=1, dtype=jnp.float32))
                    done.append(degree[-1])
        degree = sum(degree)

        mine, theirs = sums
        if ships:
            mine, theirs = mine + back[:rows], theirs + back[rows:]
        partner = exchange(theirs)
        square = mine + partner[:rows]
        col_degree = theirs[rows : rows + 1] + partner[rows : rows + 1]
        tile = adj_tile.astype(jnp.float32)
        lower = jnp.minimum(degree[:, None], col_degree)
        intersection = (square + tile) / (lower + 1.0 - tile)
        return (intersection, degree)

    return shards


def solution(mesh):
    in_specs = (
        P(("parts", "row"), None),
        P(None, ("parts", "row"), None),
        P(("parts", "row"), None),
    )
    out_specs = (P(("parts", "row"), None), P(("parts", "row")))
    return jax.shard_map(
        make_shards(mesh.shape["row"]), mesh=mesh, in_specs=in_specs, out_specs=out_specs, check_vma=False
    )
```

```python
import functools

import jax
import jax.numpy as jnp
import numpy as np
from jax import lax
from jax.experimental import pallas as pl
from jax.experimental.pallas import tpu as pltpu
from jax.sharding import PartitionSpec as P

CORES = 2
ONES = 16
SHIPS = False
SLOTS = 1
MOST = 2
ABSORB_FROM = 3
PER_LENT = 4
EARLY = 1
REST_AT = 2
DEGREE_PARTS = 4
DEGREE_AT = 2
HELP_AT = (3, 4)
LEND_AFTER = 1
TILE = 128
SHORT = pl.CostEstimate(flops=0, bytes_accessed=1024, transcendentals=0)
VMEM_LIMIT = 10 * 1024 * 1024
LEND_LIMIT = 44 * 1024 * 1024


def chip_cycle(chips):
    wide = 1
    while (2 * wide) ** 2 <= chips:
        wide *= 2
    high = chips // wide
    if wide == 1 or high % 2 or wide * high != chips:
        return list(range(chips))
    walk = [(0, 0)]
    for i in range(high):
        line = range(1, wide)
        walk += [(i, j) for j in (line if i % 2 == 0 else reversed(line))]
    walk += [(i, 0) for i in range(high - 1, 0, -1)]
    walk = walk[:1] + walk[:0:-1]
    return [i * wide + j for i, j in walk]


def make_rounds(chips, ships):
    count = 6 if ships else chips - 1
    main = [[("own", 0)] * 4] + [[("main", r)] * 4 for r in range(1, count)]
    turns = [{"main": sources} for sources in main]
    if ships:
        main[1][3] = ("own", 1)
        main[2][0] = ("ship", 0)
        main[3][0] = ("ship", 1)
        main[3][1] = ("ch", 1)
        main[4][1] = ("ch", 2)
        for r, source in ((0, ("own", 0)), (1, ("main", 1)), (2, ("main", 2)), (4, ("main", 4))):
            turns[r]["ch"] = [source] * 4
    return turns


def make_route(chips, port, r):
    if port == "main":
        return {p: (p + 1) % chips for p in range(chips)}
    return {1: 6, 5: 2} if r == 3 else {6: 1, 2: 5}


def trace_blocks(chips, turns):
    held = {("own", s): [(p, s) for p in range(chips)] for s in range(2)}
    corner = [p % 4 == 0 for p in range(chips)]
    for k, ahead in enumerate((1, 6)):
        held["ship", k] = [((p + ahead) % chips, 0) if corner[p] else None for p in range(chips)]
    for r, turn in enumerate(turns, 1):
        for port, sources in turn.items():
            held[port, r] = [None] * chips
            for p, q in make_route(chips, port, r).items():
                source = sources[p % 4]
                held[port, r][q] = None if source[0] == "ship" else held[source][p]
    return held


def lend_kernel(sizes, first, depth, where, rows_ref, *refs):
    sems = refs[-1]
    copies = []
    for part, size in enumerate(sizes):
        for k in range(size):
            unit = sum(sizes[:part]) + k
            start = pl.multiple_of(where[first + unit] * depth, 128)
            copies.append(
                pltpu.make_async_copy(
                    rows_ref.at[:, pl.ds(start, depth)],
                    refs[part].at[:, pl.ds(k * depth, depth)],
                    sems.at[unit],
                )
            )
    for copy in copies:
        copy.start()
    for copy in copies:
        copy.wait()


def lend(where, adj_rows, sizes, first, depth):
    rows = adj_rows.shape[0]
    return pl.pallas_call(
        functools.partial(lend_kernel, sizes, first, depth),
        in_specs=[pl.BlockSpec(memory_space=pltpu.SMEM), pl.BlockSpec(memory_space=pl.ANY)],
        out_specs=[pl.BlockSpec(memory_space=pltpu.VMEM)] * len(sizes),
        out_shape=[jax.ShapeDtypeStruct((rows, size * depth), adj_rows.dtype) for size in sizes],
        scratch_shapes=[pltpu.SemaphoreType.DMA((sum(sizes),))],
        compiler_params=pltpu.CompilerParams(vmem_limit_bytes=LEND_LIMIT),
        cost_estimate=SHORT,
        name="lend",
    )(where, adj_rows)


def absorb_kernel(count, flags, rows, first, where, *refs):
    own, other, slab = (refs[k * count : (k + 1) * count] for k in range(3))
    mine_out, theirs_out = refs[-2:]
    total = None
    for k in range(count):
        ones = jnp.ones((ONES, own[k].shape[1]), own[k].dtype)
        left = jnp.concatenate([own[k][...], other[k][...], ones], axis=0)
        product = jnp.dot(left, slab[k][...], preferred_element_type=jnp.float32)
        if flags[k] is not None:
            product = jnp.where(where[flags[k]] > 0, product, 0.0)
        total = product if total is None else total + product
    mine, theirs = total[:rows], total[rows:]
    if not first:
        mine_in, theirs_in = refs[3 * count : 3 * count + 2]
        mine, theirs = mine + mine_in[...], theirs + theirs_in[...]
    mine_out[...] = mine
    theirs_out[...] = theirs


def absorb(where, adj_rows, borrowed, slabs, units, flags, sums, cuts=1, cut=0):
    count = len(slabs)
    rows = adj_rows.shape[0]
    depth, width = slabs[0].shape

    def own(k):
        return pl.BlockSpec((rows, depth), lambda g, where: (0, where[2 + units[k]] * cuts + cut))

    def other(k):
        return pl.BlockSpec((rows, depth), lambda g, where: (0, units[k] % PER_LENT * cuts + cut))

    def whole(shape):
        return pl.BlockSpec(shape, lambda g, where: (0, 0))

    shapes = [(rows, width), (rows + ONES, width)]
    first = sums is None
    operands = [adj_rows] * count + [borrowed[unit // PER_LENT] for unit in units] + list(slabs)
    in_specs = [own(k) for k in range(count)] + [other(k) for k in range(count)]
    in_specs += [whole((depth, width))] * count
    if not first:
        operands += list(sums)
        in_specs += [whole(shape) for shape in shapes]
    at = 1 + 3 * count
    return pl.pallas_call(
        functools.partial(absorb_kernel, count, flags, rows, first),
        grid_spec=pltpu.PrefetchScalarGridSpec(
            num_scalar_prefetch=1,
            grid=(1,),
            in_specs=in_specs,
            out_specs=[whole(shape) for shape in shapes],
        ),
        out_shape=[jax.ShapeDtypeStruct(shape, jnp.float32) for shape in shapes],
        input_output_aliases={} if first else {at: 0, at + 1: 1},
        compiler_params=pltpu.CompilerParams(vmem_limit_bytes=VMEM_LIMIT),
        cost_estimate=SHORT,
        name="absorb",
    )(where, *operands)


def pick_kernel(choices, n_in, where, *refs):
    outs = refs[n_in:]
    for out, by_kind in zip(outs, choices):
        for source in sorted(set(by_kind), key=str):
            kinds = [kind for kind, chosen in enumerate(by_kind) if chosen == source]
            here = where[1] == kinds[0]
            for kind in kinds[1:]:
                here = here | (where[1] == kind)

            def send(out=out, source=source):
                if isinstance(source, int):
                    out[...] = refs[source][...]
                    return
                left = jnp.concatenate([refs[source[0]][...], refs[source[1]][...]], axis=0)
                for i in range(left.shape[0] // TILE):
                    for k in range(left.shape[1] // TILE):
                        out[k * TILE : (k + 1) * TILE, i * TILE : (i + 1) * TILE] = left[
                            i * TILE : (i + 1) * TILE, k * TILE : (k + 1) * TILE
                        ]

            pl.when(here)(send)


def pick(where, operands, specs, choices, shape):
    return pl.pallas_call(
        functools.partial(pick_kernel, choices, len(operands)),
        grid_spec=pltpu.PrefetchScalarGridSpec(
            num_scalar_prefetch=1,
            grid=(1,),
            in_specs=specs,
            out_specs=[pl.BlockSpec(shape.shape, lambda g, where: (0, 0))] * len(choices),
        ),
        out_shape=[shape] * len(choices),
        compiler_params=pltpu.CompilerParams(vmem_limit_bytes=VMEM_LIMIT),
        cost_estimate=SHORT,
        name="pick",
    )(where, *operands)


def help_kernel(rows, first, where, *refs):
    mine_out, theirs_out, left = refs[-3:]
    packed, slab = refs[:2]
    if first:
        mine_out[...] = jnp.zeros_like(mine_out)
        theirs_out[...] = jnp.zeros_like(theirs_out)
    else:
        mine_out[...] = refs[2][...]
        theirs_out[...] = refs[3][...]

    @pl.when(where[1] == 1)
    def _():
        depth, width = packed.shape
        for i in range(width // TILE):
            for k in range(depth // TILE):
                left[i * TILE : (i + 1) * TILE, k * TILE : (k + 1) * TILE] = packed[
                    k * TILE : (k + 1) * TILE, i * TILE : (i + 1) * TILE
                ]
        left[width:, :] = jnp.ones((ONES, depth), left.dtype)
        product = jnp.dot(left[...], slab[...], preferred_element_type=jnp.float32)
        mine_out[...] += product[:rows]
        theirs_out[...] += product[rows:]


def help_corner(where, packed, slab, rows, sums):
    depth, width = packed.shape
    shapes = [(rows, width), (rows + ONES, width)]
    first = sums is None
    operands = [packed, slab] + ([] if first else list(sums))

    def whole(shape):
        return pl.BlockSpec(shape, lambda g, where: (0, 0))

    return pl.pallas_call(
        functools.partial(help_kernel, rows, first),
        grid_spec=pltpu.PrefetchScalarGridSpec(
            num_scalar_prefetch=1,
            grid=(1,),
            in_specs=[whole((depth, width))] * 2 + ([] if first else [whole(s) for s in shapes]),
            out_specs=[whole(shape) for shape in shapes],
            scratch_shapes=[pltpu.VMEM((width + ONES, depth), packed.dtype)],
        ),
        out_shape=[jax.ShapeDtypeStruct(shape, jnp.float32) for shape in shapes],
        compiler_params=pltpu.CompilerParams(vmem_limit_bytes=VMEM_LIMIT),
        cost_estimate=SHORT,
        name="help",
    )(where, *operands)


def make_shards(n_row):
    chips = n_row // CORES
    cycle = chip_cycle(chips)
    place = {chip: k for k, chip in enumerate(cycle)}

    def walk(d):
        p = place[d // CORES]
        return p if d % CORES == 0 else chips - 1 - p

    def device(p, c):
        return cycle[p if c == 0 else chips - 1 - p] * CORES + c

    def pairs(route):
        return [(device(p, c), device(q, c)) for p, q in route.items() for c in range(CORES)]

    swap = [(d, d ^ 1) for d in range(n_row)]

    def shards(adj_rows, adj_panel, adj_tile):
        rows = adj_rows.shape[0]
        _, depth, width = adj_panel.shape
        ships = SHIPS and chips == 8 and 2 * rows == width and width % TILE == 0 and depth % TILE == 0
        turns = make_rounds(chips, ships)
        blocks = trace_blocks(chips, turns)
        rounds = len(turns)
        halves = range(CORES)
        cuts = 2 if depth % 256 == 0 and not ships else 1

        groups = [[("own", 0)]] + [[(port, r) for port in turn] for r, turn in enumerate(turns, 1)]
        sources = [source for group in groups for source in group]
        if ships:
            sources = [("ship", 0), ("ship", 1)] + sources
        units, flags = {}, {}
        table = [[d % CORES, walk(d) % 4] for d in range(n_row)]
        for k, source in enumerate(sources):
            units[source] = [CORES * k + j for j in halves]
            for d in range(n_row):
                c = d % CORES
                p, other = blocks[source][walk(d)] or (walk(d), 0)
                owner = device(p, c) // CORES
                table[d] += [(c ^ other) * n_row + owner * CORES + (c ^ j) for j in halves]
        n_units = CORES * len(sources)
        table = [table[d] + table[d ^ 1][2:] for d in range(n_row)]
        for source in sources:
            flags[source] = None
            if source[0] == "main" and None in blocks[source]:
                flags[source] = len(table[0])
                for d in range(n_row):
                    table[d].append(int(blocks[source][walk(d)] is not None))
        me = lax.axis_index("row")
        where = jnp.asarray(np.array(table, np.int32))[me]
        core = lax.rem(me, CORES)

        def tie(values, others):
            return lax.optimization_barrier((values, others))[0]

        def exchange(value):
            return lax.ppermute(value, "row", swap)

        def depart(turn, j):
            sending = {}
            for port, chosen in turn.items():
                kinds = sorted(set(chosen))
                pieces = [(packed if source[0] == "ship" else slab)[source][j] for source in kinds]
                if len(kinds) == 1:
                    sending[port] = pieces[0]
                    continue
                specs = [pl.BlockSpec((depth, width), lambda g, where: (0, 0))] * len(pieces)
                choices = [[kinds.index(source) for source in chosen]]
                shape = jax.ShapeDtypeStruct((depth, width), adj_panel.dtype)
                sending[port] = pick(where, pieces, specs, choices, shape)[0]
            return sending

        def pack(source):
            shape = jax.ShapeDtypeStruct((depth, width), adj_panel.dtype)
            result = []
            for unit in units[source]:
                specs = [
                    pl.BlockSpec((rows, depth), lambda g, where, unit=unit: (0, where[2 + unit])),
                    pl.BlockSpec((rows, depth), lambda g, where, unit=unit: (0, unit % PER_LENT)),
                ]
                result += pick(where, [adj_rows, borrowed[unit // PER_LENT]], specs, [[(0, 1)] * 4], shape)
            return result

        here = lax.dynamic_index_in_dim(adj_panel, core, 0, keepdims=False)
        there = lax.dynamic_index_in_dim(adj_panel, 1 - core, 0, keepdims=False)
        slab = {("own", 0): [here, exchange(there)]}
        if ships:
            slab["own", 1] = [there, exchange(here)]
        sizes = [min(PER_LENT, n_units - k) for k in range(0, n_units, PER_LENT)]
        lent = lend(where, tie(adj_rows, slab["own", 0][LEND_AFTER]), sizes, 2 + n_units, depth)
        borrowed = [exchange(part) for part in lent[:EARLY]]
        packed = {("ship", k): pack(("ship", k)) for k in range(2)} if ships else {}
        sums, helped = None, None
        degree = []
        due = [(0, j) for j in halves]
        stretch = adj_rows.shape[1] // DEGREE_PARTS
        past = []
        for r in range(1, rounds + 2):
            for port in turns[r - 1] if r <= rounds else ():
                slab[port, r] = []
            for j in halves:
                at = r - 1
                if at > 0 and r <= rounds and len(past) >= SLOTS:
                    arrived = tie([slab[port, at][j] for port in turns[at - 1]], past[-SLOTS])
                    for port, piece in zip(turns[at - 1], arrived):
                        slab[port, at][j] = piece
                if r <= rounds:
                    sending = depart(turns[r - 1], j)
                    if r == rounds and j == 1 and cuts > 1:
                        piece, size = sending["main"], depth // cuts
                        last = [
                            lax.ppermute(piece[k * size : (k + 1) * size], "row", pairs(make_route(chips, "main", r)))
                            for k in range(cuts)
                        ]
                        slab["main", r].append(last)
                        sending = {}
                    for port, piece in sending.items():
                        slab[port, r].append(lax.ppermute(piece, "row", pairs(make_route(chips, port, r))))
                    if r == REST_AT and j == 0:
                        borrowed += [exchange(part) for part in tie(lent[EARLY:], list(sending.values()))]
                if at == 0:
                    continue
                gate = [slab[port, at][j] for port in turns[at - 1]]
                if isinstance(gate[0], list):
                    gate = [gate[0][0]]
                if r <= rounds:
                    gate = [gate, list(sending.values())]
                done = []
                past.append(done)
                due.append((at, j))
                if ships and at in HELP_AT:
                    beside = slab["own", 0] if at == HELP_AT[0] else slab["ch", 1]
                    helped = help_corner(where, slab["main", at][j], tie(beside[j], gate), rows, helped)
                    done.append(helped)
                    if (at, j) == (HELP_AT[1], 1):
                        back = lax.ppermute(jnp.concatenate(helped, axis=0), "row", pairs({1: 0, 5: 4}))
                if at >= ABSORB_FROM:
                    now = tie(adj_rows, gate)
                    for _ in range(MOST if r <= rounds else len(due)):
                        if due:
                            t, part = due.pop(0)
                            if isinstance(slab[groups[t][0]][part], list):
                                unit = units[groups[t][0]][part]
                                for k, piece in enumerate(last):
                                    rows_now = adj_rows
                                    sums = absorb(where, rows_now, borrowed, [piece], [unit], [None], sums, cuts, k)
                                continue
                            sums = absorb(
                                where,
                                now,
                                borrowed,
                                tie([slab[source][part] for source in groups[t]], gate),
                                [units[source][part] for source in groups[t]],
                                [flags[source] for source in groups[t]],
                                sums,
                            )
                            done.append(sums)
                if at >= DEGREE_AT and len(degree) < DEGREE_PARTS:
                    k = len(degree) * stretch
                    part = lax.slice_in_dim(tie(adj_rows, gate), k, k + stretch, axis=1)
                    degree.append(jnp.sum(part, axis=1, dtype=jnp.float32))
                    done.append(degree[-1])
        degree = sum(degree)

        mine, theirs = sums
        if ships:
            mine, theirs = mine + back[:rows], theirs + back[rows:]
        partner = exchange(theirs)
        square = mine + partner[:rows]
        col_degree = theirs[rows : rows + 1] + partner[rows : rows + 1]
        tile = adj_tile.astype(jnp.float32)
        lower = jnp.minimum(degree[:, None], col_degree)
        intersection = (square + tile) / (lower + 1.0 - tile)
        return (intersection, degree)

    return shards


def solution(mesh):
    in_specs = (
        P(("parts", "row"), None),
        P(None, ("parts", "row"), None),
        P(("parts", "row"), None),
    )
    out_specs = (P(("parts", "row"), None), P(("parts", "row")))
    return jax.shard_map(
        make_shards(mesh.shape["row"]), mesh=mesh, in_specs=in_specs, out_specs=out_specs, check_vma=False
    )
```

```python
import functools

import jax
import jax.numpy as jnp
import numpy as np
from jax import lax
from jax.experimental import pallas as pl
from jax.experimental.pallas import tpu as pltpu
from jax.sharding import PartitionSpec as P

CORES = 2
ONES = 16
SHIPS = False
SLOTS = 1
MOST = 2
ABSORB_FROM = 3
PER_LENT = 8
EARLY = 1
REST_AT = 2
DEGREE_PARTS = 4
DEGREE_AT = 2
HELP_AT = (3, 4)
LEND_AFTER = 1
TILE = 128
SHORT = pl.CostEstimate(flops=0, bytes_accessed=1024, transcendentals=0)
VMEM_LIMIT = 10 * 1024 * 1024
LEND_LIMIT = 44 * 1024 * 1024


def chip_cycle(chips):
    wide = 1
    while (2 * wide) ** 2 <= chips:
        wide *= 2
    high = chips // wide
    if wide == 1 or high % 2 or wide * high != chips:
        return list(range(chips))
    walk = [(0, 0)]
    for i in range(high):
        line = range(1, wide)
        walk += [(i, j) for j in (line if i % 2 == 0 else reversed(line))]
    walk += [(i, 0) for i in range(high - 1, 0, -1)]
    walk = walk[:1] + walk[:0:-1]
    return [i * wide + j for i, j in walk]


def make_rounds(chips, ships):
    count = 6 if ships else chips - 1
    main = [[("own", 0)] * 4] + [[("main", r)] * 4 for r in range(1, count)]
    turns = [{"main": sources} for sources in main]
    if ships:
        main[1][3] = ("own", 1)
        main[2][0] = ("ship", 0)
        main[3][0] = ("ship", 1)
        main[3][1] = ("ch", 1)
        main[4][1] = ("ch", 2)
        for r, source in ((0, ("own", 0)), (1, ("main", 1)), (2, ("main", 2)), (4, ("main", 4))):
            turns[r]["ch"] = [source] * 4
    return turns


def make_route(chips, port, r):
    if port == "main":
        return {p: (p + 1) % chips for p in range(chips)}
    return {1: 6, 5: 2} if r == 3 else {6: 1, 2: 5}


def trace_blocks(chips, turns):
    held = {("own", s): [(p, s) for p in range(chips)] for s in range(2)}
    corner = [p % 4 == 0 for p in range(chips)]
    for k, ahead in enumerate((1, 6)):
        held["ship", k] = [((p + ahead) % chips, 0) if corner[p] else None for p in range(chips)]
    for r, turn in enumerate(turns, 1):
        for port, sources in turn.items():
            held[port, r] = [None] * chips
            for p, q in make_route(chips, port, r).items():
                source = sources[p % 4]
                held[port, r][q] = None if source[0] == "ship" else held[source][p]
    return held


def lend_kernel(sizes, first, depth, where, rows_ref, *refs):
    sems = refs[-1]
    copies = []
    for part, size in enumerate(sizes):
        for k in range(size):
            unit = sum(sizes[:part]) + k
            start = pl.multiple_of(where[first + unit] * depth, 128)
            copies.append(
                pltpu.make_async_copy(
                    rows_ref.at[:, pl.ds(start, depth)],
                    refs[part].at[:, pl.ds(k * depth, depth)],
                    sems.at[unit],
                )
            )
    for copy in copies:
        copy.start()
    for copy in copies:
        copy.wait()


def lend(where, adj_rows, sizes, first, depth):
    rows = adj_rows.shape[0]
    return pl.pallas_call(
        functools.partial(lend_kernel, sizes, first, depth),
        in_specs=[pl.BlockSpec(memory_space=pltpu.SMEM), pl.BlockSpec(memory_space=pl.ANY)],
        out_specs=[pl.BlockSpec(memory_space=pltpu.VMEM)] * len(sizes),
        out_shape=[jax.ShapeDtypeStruct((rows, size * depth), adj_rows.dtype) for size in sizes],
        scratch_shapes=[pltpu.SemaphoreType.DMA((sum(sizes),))],
        compiler_params=pltpu.CompilerParams(vmem_limit_bytes=LEND_LIMIT),
        cost_estimate=SHORT,
        name="lend",
    )(where, adj_rows)


def absorb_kernel(count, flags, rows, first, where, *refs):
    own, other, slab = (refs[k * count : (k + 1) * count] for k in range(3))
    mine_out, theirs_out = refs[-2:]
    total = None
    for k in range(count):
        ones = jnp.ones((ONES, own[k].shape[1]), own[k].dtype)
        left = jnp.concatenate([own[k][...], other[k][...], ones], axis=0)
        product = jnp.dot(left, slab[k][...], preferred_element_type=jnp.float32)
        if flags[k] is not None:
            product = jnp.where(where[flags[k]] > 0, product, 0.0)
        total = product if total is None else total + product
    mine, theirs = total[:rows], total[rows:]
    if not first:
        mine_in, theirs_in = refs[3 * count : 3 * count + 2]
        mine, theirs = mine + mine_in[...], theirs + theirs_in[...]
    mine_out[...] = mine
    theirs_out[...] = theirs


def absorb(where, adj_rows, borrowed, slabs, units, flags, sums):
    count = len(slabs)
    rows = adj_rows.shape[0]
    depth, width = slabs[0].shape

    def own(k):
        return pl.BlockSpec((rows, depth), lambda g, where: (0, where[2 + units[k]]))

    def other(k):
        return pl.BlockSpec((rows, depth), lambda g, where: (0, units[k] % PER_LENT))

    def whole(shape):
        return pl.BlockSpec(shape, lambda g, where: (0, 0))

    shapes = [(rows, width), (rows + ONES, width)]
    first = sums is None
    operands = [adj_rows] * count + [borrowed[unit // PER_LENT] for unit in units] + list(slabs)
    in_specs = [own(k) for k in range(count)] + [other(k) for k in range(count)]
    in_specs += [whole((depth, width))] * count
    if not first:
        operands += list(sums)
        in_specs += [whole(shape) for shape in shapes]
    at = 1 + 3 * count
    return pl.pallas_call(
        functools.partial(absorb_kernel, count, flags, rows, first),
        grid_spec=pltpu.PrefetchScalarGridSpec(
            num_scalar_prefetch=1,
            grid=(1,),
            in_specs=in_specs,
            out_specs=[whole(shape) for shape in shapes],
        ),
        out_shape=[jax.ShapeDtypeStruct(shape, jnp.float32) for shape in shapes],
        input_output_aliases={} if first else {at: 0, at + 1: 1},
        compiler_params=pltpu.CompilerParams(vmem_limit_bytes=VMEM_LIMIT),
        cost_estimate=SHORT,
        name="absorb",
    )(where, *operands)


def pick_kernel(choices, n_in, where, *refs):
    outs = refs[n_in:]
    for out, by_kind in zip(outs, choices):
        for source in sorted(set(by_kind), key=str):
            kinds = [kind for kind, chosen in enumerate(by_kind) if chosen == source]
            here = where[1] == kinds[0]
            for kind in kinds[1:]:
                here = here | (where[1] == kind)

            def send(out=out, source=source):
                if isinstance(source, int):
                    out[...] = refs[source][...]
                    return
                left = jnp.concatenate([refs[source[0]][...], refs[source[1]][...]], axis=0)
                for i in range(left.shape[0] // TILE):
                    for k in range(left.shape[1] // TILE):
                        out[k * TILE : (k + 1) * TILE, i * TILE : (i + 1) * TILE] = left[
                            i * TILE : (i + 1) * TILE, k * TILE : (k + 1) * TILE
                        ]

            pl.when(here)(send)


def pick(where, operands, specs, choices, shape):
    return pl.pallas_call(
        functools.partial(pick_kernel, choices, len(operands)),
        grid_spec=pltpu.PrefetchScalarGridSpec(
            num_scalar_prefetch=1,
            grid=(1,),
            in_specs=specs,
            out_specs=[pl.BlockSpec(shape.shape, lambda g, where: (0, 0))] * len(choices),
        ),
        out_shape=[shape] * len(choices),
        compiler_params=pltpu.CompilerParams(vmem_limit_bytes=VMEM_LIMIT),
        cost_estimate=SHORT,
        name="pick",
    )(where, *operands)


def help_kernel(rows, first, where, *refs):
    mine_out, theirs_out, left = refs[-3:]
    packed, slab = refs[:2]
    if first:
        mine_out[...] = jnp.zeros_like(mine_out)
        theirs_out[...] = jnp.zeros_like(theirs_out)
    else:
        mine_out[...] = refs[2][...]
        theirs_out[...] = refs[3][...]

    @pl.when(where[1] == 1)
    def _():
        depth, width = packed.shape
        for i in range(width // TILE):
            for k in range(depth // TILE):
                left[i * TILE : (i + 1) * TILE, k * TILE : (k + 1) * TILE] = packed[
                    k * TILE : (k + 1) * TILE, i * TILE : (i + 1) * TILE
                ]
        left[width:, :] = jnp.ones((ONES, depth), left.dtype)
        product = jnp.dot(left[...], slab[...], preferred_element_type=jnp.float32)
        mine_out[...] += product[:rows]
        theirs_out[...] += product[rows:]


def help_corner(where, packed, slab, rows, sums):
    depth, width = packed.shape
    shapes = [(rows, width), (rows + ONES, width)]
    first = sums is None
    operands = [packed, slab] + ([] if first else list(sums))

    def whole(shape):
        return pl.BlockSpec(shape, lambda g, where: (0, 0))

    return pl.pallas_call(
        functools.partial(help_kernel, rows, first),
        grid_spec=pltpu.PrefetchScalarGridSpec(
            num_scalar_prefetch=1,
            grid=(1,),
            in_specs=[whole((depth, width))] * 2 + ([] if first else [whole(s) for s in shapes]),
            out_specs=[whole(shape) for shape in shapes],
            scratch_shapes=[pltpu.VMEM((width + ONES, depth), packed.dtype)],
        ),
        out_shape=[jax.ShapeDtypeStruct(shape, jnp.float32) for shape in shapes],
        compiler_params=pltpu.CompilerParams(vmem_limit_bytes=VMEM_LIMIT),
        cost_estimate=SHORT,
        name="help",
    )(where, *operands)


def make_shards(n_row):
    chips = n_row // CORES
    cycle = chip_cycle(chips)
    place = {chip: k for k, chip in enumerate(cycle)}

    def walk(d):
        p = place[d // CORES]
        return p if d % CORES == 0 else chips - 1 - p

    def device(p, c):
        return cycle[p if c == 0 else chips - 1 - p] * CORES + c

    def pairs(route):
        return [(device(p, c), device(q, c)) for p, q in route.items() for c in range(CORES)]

    swap = [(d, d ^ 1) for d in range(n_row)]

    def shards(adj_rows, adj_panel, adj_tile):
        rows = adj_rows.shape[0]
        _, depth, width = adj_panel.shape
        ships = SHIPS and chips == 8 and 2 * rows == width and width % TILE == 0 and depth % TILE == 0
        turns = make_rounds(chips, ships)
        blocks = trace_blocks(chips, turns)
        rounds = len(turns)
        halves = range(CORES)

        groups = [[("own", 0)]] + [[(port, r) for port in turn] for r, turn in enumerate(turns, 1)]
        sources = [source for group in groups for source in group]
        if ships:
            sources = [("ship", 0), ("ship", 1)] + sources
        units, flags = {}, {}
        table = [[d % CORES, walk(d) % 4] for d in range(n_row)]
        for k, source in enumerate(sources):
            units[source] = [CORES * k + j for j in halves]
            for d in range(n_row):
                c = d % CORES
                p, other = blocks[source][walk(d)] or (walk(d), 0)
                owner = device(p, c) // CORES
                table[d] += [(c ^ other) * n_row + owner * CORES + (c ^ j) for j in halves]
        n_units = CORES * len(sources)
        table = [table[d] + table[d ^ 1][2:] for d in range(n_row)]
        for source in sources:
            flags[source] = None
            if source[0] == "main" and None in blocks[source]:
                flags[source] = len(table[0])
                for d in range(n_row):
                    table[d].append(int(blocks[source][walk(d)] is not None))
        me = lax.axis_index("row")
        where = jnp.asarray(np.array(table, np.int32))[me]
        core = lax.rem(me, CORES)

        def tie(values, others):
            return lax.optimization_barrier((values, others))[0]

        def exchange(value):
            return lax.ppermute(value, "row", swap)

        def depart(turn, j):
            sending = {}
            for port, chosen in turn.items():
                kinds = sorted(set(chosen))
                pieces = [(packed if source[0] == "ship" else slab)[source][j] for source in kinds]
                if len(kinds) == 1:
                    sending[port] = pieces[0]
                    continue
                specs = [pl.BlockSpec((depth, width), lambda g, where: (0, 0))] * len(pieces)
                choices = [[kinds.index(source) for source in chosen]]
                shape = jax.ShapeDtypeStruct((depth, width), adj_panel.dtype)
                sending[port] = pick(where, pieces, specs, choices, shape)[0]
            return sending

        def pack(source):
            shape = jax.ShapeDtypeStruct((depth, width), adj_panel.dtype)
            result = []
            for unit in units[source]:
                specs = [
                    pl.BlockSpec((rows, depth), lambda g, where, unit=unit: (0, where[2 + unit])),
                    pl.BlockSpec((rows, depth), lambda g, where, unit=unit: (0, unit % PER_LENT)),
                ]
                result += pick(where, [adj_rows, borrowed[unit // PER_LENT]], specs, [[(0, 1)] * 4], shape)
            return result

        here = lax.dynamic_index_in_dim(adj_panel, core, 0, keepdims=False)
        there = lax.dynamic_index_in_dim(adj_panel, 1 - core, 0, keepdims=False)
        slab = {("own", 0): [here, exchange(there)]}
        if ships:
            slab["own", 1] = [there, exchange(here)]
        sizes = [min(PER_LENT, n_units - k) for k in range(0, n_units, PER_LENT)]
        lent = lend(where, tie(adj_rows, slab["own", 0][LEND_AFTER]), sizes, 2 + n_units, depth)
        borrowed = [exchange(part) for part in lent[:EARLY]]
        packed = {("ship", k): pack(("ship", k)) for k in range(2)} if ships else {}
        sums, helped = None, None
        degree = []
        due = [(0, j) for j in halves]
        stretch = adj_rows.shape[1] // DEGREE_PARTS
        past = []
        for r in range(1, rounds + 2):
            for port in turns[r - 1] if r <= rounds else ():
                slab[port, r] = []
            for j in halves:
                at = r - 1
                if at > 0 and len(past) >= SLOTS:
                    arrived = tie([slab[port, at][j] for port in turns[at - 1]], past[-SLOTS])
                    for port, piece in zip(turns[at - 1], arrived):
                        slab[port, at][j] = piece
                if r <= rounds:
                    sending = depart(turns[r - 1], j)
                    for port, piece in sending.items():
                        slab[port, r].append(lax.ppermute(piece, "row", pairs(make_route(chips, port, r))))
                    if r == REST_AT and j == 0:
                        borrowed += [exchange(part) for part in tie(lent[EARLY:], list(sending.values()))]
                if at == 0:
                    continue
                gate = [slab[port, at][j] for port in turns[at - 1]]
                if r <= rounds:
                    gate = [gate, list(sending.values())]
                done = []
                past.append(done)
                due.append((at, j))
                if ships and at in HELP_AT:
                    beside = slab["own", 0] if at == HELP_AT[0] else slab["ch", 1]
                    helped = help_corner(where, slab["main", at][j], tie(beside[j], gate), rows, helped)
                    done.append(helped)
                    if (at, j) == (HELP_AT[1], 1):
                        back = lax.ppermute(jnp.concatenate(helped, axis=0), "row", pairs({1: 0, 5: 4}))
                if at >= ABSORB_FROM:
                    now = tie(adj_rows, gate)
                    for _ in range(MOST if r <= rounds else len(due)):
                        if due:
                            t, part = due.pop(0)
                            sums = absorb(
                                where,
                                now,
                                borrowed,
                                tie([slab[source][part] for source in groups[t]], gate),
                                [units[source][part] for source in groups[t]],
                                [flags[source] for source in groups[t]],
                                sums,
                            )
                            done.append(sums)
                if at >= DEGREE_AT and len(degree) < DEGREE_PARTS:
                    k = len(degree) * stretch
                    part = lax.slice_in_dim(tie(adj_rows, gate), k, k + stretch, axis=1)
                    degree.append(jnp.sum(part, axis=1, dtype=jnp.float32))
                    done.append(degree[-1])
        degree = sum(degree)

        mine, theirs = sums
        if ships:
            mine, theirs = mine + back[:rows], theirs + back[rows:]
        partner = exchange(theirs)
        square = mine + partner[:rows]
        col_degree = theirs[rows : rows + 1] + partner[rows : rows + 1]
        tile = adj_tile.astype(jnp.float32)
        lower = jnp.minimum(degree[:, None], col_degree)
        intersection = (square + tile) / (lower + 1.0 - tile)
        return (intersection, degree)

    return shards


def solution(mesh):
    in_specs = (
        P(("parts", "row"), None),
        P(None, ("parts", "row"), None),
        P(("parts", "row"), None),
    )
    out_specs = (P(("parts", "row"), None), P(("parts", "row")))
    return jax.shard_map(
        make_shards(mesh.shape["row"]), mesh=mesh, in_specs=in_specs, out_specs=out_specs, check_vma=False
    )
```
